256 devices in a mesh: dp: 32 (over x, y, core), seq: 8 (over z).
Axes of the slice: x: 4, y: 4, z: 8, core: 2. Of those that a mesh axis runs over, the one named last changes fastest.
Arguments:
- history: bfloat16 [262144, 1024], P(('dp', 'seq')), may hold values from -6 to 6
- hist_dest: int32 [262144, 1], P(('dp', 'seq')), may hold values from 0 to 31; in each aligned block of 1024 rows (0 to 1023, 1024 to 2047, ...) at most 64 rows name the same one
- hist_user: int32 [262144], P(('dp', 'seq')), may hold values from 0 to 15
- candidates: bfloat16 [8192, 1024], P(('dp', 'seq')), may hold values from -6 to 6
- cand_user: int32 [8192], P('dp'), may hold values from 0 to 15
- w_qu: bfloat16 [1024, 2048], replicated, may hold values from -0.1875 to 0.1875
- w_kv: bfloat16 [1024, 2048], replicated, may hold values from -0.1875 to 0.1875
- w_out: bfloat16 [1024, 1024], replicated, may hold values from -0.1875 to 0.1875
Outputs:
- scored: float32 [8192, 1024], P(('dp', 'seq'))
The draws below stay inside these ranges and needn't reach their ends.
Inputs may be any that keep to these rules, and one draw needn't show every extreme that they name: `hist_dest`: among the rows of one device, no dp group is named more than 64 times; in some devices one group is named exactly 64 times.
All inputs are finite; a program needn't handle non-finite values.
Results may differ from the reference program's by a relative error of at most 0.003.
Values may be sent and summed in bfloat16 or wider, within the bound.
A program may use at most 128 MiB of HBM per device.

```python
import math
import jax
import jax.numpy as jnp
import numpy as np
from jax import lax

D = 1024
HEAD_TOTAL = 8
TOK_H = 1024
C_DEV = 32
U_GRP = 16
CAP = 64
HIST = 262144
CAND = 8192
N_DP = 32
N_SEQ = 8


def touch_ends(drawn, stream_key, low, top_value):
    longest = drawn.shape.index(max(drawn.shape))
    spots = []
    for shift in (0, 1):
        where = [jax.random.randint(jax.random.fold_in(stream_key, axis), (), 0, length) for axis, length in enumerate(drawn.shape)]
        where[longest] = (where[longest] + shift) % drawn.shape[longest]
        spots.append(tuple(where))
    return drawn.at[spots[0]].set(low).at[spots[1]].set(top_value)


def steps_of(key, shape, split, least, top_value):
    def one(dim, blocks):
        draws = jax.random.uniform(jax.random.fold_in(jax.random.fold_in(key, 6), dim), (blocks,), jnp.float32, least / len(split), top_value / len(split))
        return jnp.repeat(jnp.exp(draws), shape[dim] // blocks).reshape((-1,) + (1,) * (len(shape) - dim - 1))

    loudness = one(*split[0])
    for cut in split[1:]:
        loudness = loudness * one(*cut)
    return loudness


def rank_table(amount, skew):
    portions = [(1 << 20) // math.isqrt(rank ** skew) + 1 for rank in range(1, amount + 1)]
    deviation = 1 + sum(portions) // (1 << 30)
    return np.cumsum(np.array([max(1, weight // deviation) for weight in portions]))


def ranked(stream_key, shape, count, slope):
    listing = rank_table(count, slope)
    lot = jax.random.randint(jax.random.fold_in(stream_key, 1), shape, 0, int(listing[count - 1]))
    standing = jnp.searchsorted(jnp.asarray(listing, jnp.int32), lot, side="right")
    return jax.random.permutation(jax.random.fold_in(stream_key, 2), count)[standing].astype(jnp.int32)


def routed_block(own_key, own, number, rows, count, top, limit, lean):
    ranking = jax.random.permutation(own_key, count)
    heavy_load, common = shares(count, rows * top, limit, lean, True), shares(count, rows * top, limit, lean, False)
    places = jnp.arange(count)

    def named(lengths, offset_by):
        used = int((lengths > 0).sum())
        fixed = max(1, used // 4)
        shifted = fixed + (places - fixed + offset_by * (used - fixed)) % max(1, count - fixed)
        return jnp.zeros((count,), jnp.int32).at[ranking[jnp.where(places < fixed, places, shifted)]].set(jnp.asarray(lengths, jnp.int32))

    lengths = jnp.where(number % 4 == 0, named(heavy_load, number // 4), named(common, number - number // 4 - 1))
    mixed = jax.random.permutation(jax.random.fold_in(own, 3), count)
    source_of, sink = mixed[0:count // 2 * 2:2], mixed[1:count // 2 * 2:2]
    room = jnp.minimum(lengths[source_of] - 1, limit - lengths[sink]) // 2
    room = jnp.where((source_of == ranking[0]) | (sink == ranking[0]) | (lengths[sink] == 0), 0, jnp.maximum(room, 0))
    shifted = jax.random.randint(jax.random.fold_in(own, 4), (count // 2,), 0, 1 << 20) % (room + 1)
    lengths = lengths.at[source_of].add(-shifted).at[sink].add(shifted)
    members = jnp.searchsorted(jnp.cumsum(lengths), jnp.arange(rows * top), side="right").astype(jnp.int32)
    grid = members.reshape(top, rows).T
    grid = grid[jax.random.permutation(jax.random.fold_in(own, 1), rows)]
    offset_by = jax.random.randint(jax.random.fold_in(own, 2), (rows, 1), 0, top)
    return jnp.take_along_axis(grid, (jnp.arange(top)[None, :] + offset_by) % top, axis=1)


def shares(number_of, total, bound, lean, full):
    portions = [(1 << 20) // math.isqrt(rank ** lean) + 1 for rank in range(1, number_of + 1)]
    largest = bound if full else min(bound, max(-(-total // number_of), total * portions[0] // sum(portions)))
    least = 1 if total - largest >= number_of - 1 else 0
    given, surplus = [largest] + [least] * (number_of - 1), total - largest - least * (number_of - 1)
    while surplus > 0:
        free = [i for i in range(1, number_of) if given[i] < largest] or [i for i in range(1, number_of) if given[i] < bound]
        mass, remaining = sum([portions[i] for i in free]), surplus
        for i in free:
            extra = min(bound - given[i], max(1, remaining * portions[i] // mass), surplus)
            given[i] = given[i] + extra
            surplus = surplus - extra
    return np.array(given)


def bell_draw(own_key, dims, width, reach, shards=(), held_as=jnp.bfloat16):
    result = width * jax.random.normal(own_key, dims, jnp.float32)
    if shards:
        result = result * steps_of(own_key, dims, shards, -0.22, 0.18)
    return jnp.clip(result, -reach, reach).astype(held_as)


def setup_inputs(seed: int = 0) -> dict:
    arg_keys = jax.random.split(jax.random.key(seed), 9)
    history = bell_draw(arg_keys[0], (HIST, D), 1.0, 6.0, ((0, 256),))
    hist_dest_keys = jax.random.split(jax.random.fold_in(arg_keys[1], 1), HIST // TOK_H)
    hist_dest_turns = jax.random.permutation(jax.random.fold_in(arg_keys[1], 3), HIST // TOK_H)
    hist_dest = jax.vmap(lambda own, number: routed_block(jax.random.fold_in(arg_keys[1], 2), own, number, TOK_H, N_DP, 1, CAP, 2))(hist_dest_keys, hist_dest_turns).reshape((HIST, 1))
    hist_user = touch_ends(ranked(arg_keys[2], (HIST,), U_GRP, 2), jax.random.fold_in(arg_keys[2], 3), 0, U_GRP - 1).astype(jnp.int32)
    candidates = bell_draw(arg_keys[3], (CAND, D), 1.0, 6.0, ((0, 256),))
    cand_user = touch_ends(jax.random.randint(arg_keys[4], (CAND,), 0, U_GRP), jax.random.fold_in(arg_keys[4], 1), 0, U_GRP - 1).astype(jnp.int32)
    w_qu = bell_draw(arg_keys[5], (D, 2 * D), D ** -0.5, 0.1875)
    w_kv = bell_draw(arg_keys[6], (D, 2 * D), D ** -0.5, 0.1875)
    w_out = bell_draw(arg_keys[7], (D, D), D ** -0.5, 0.1875)
    return dict(history=history, hist_dest=hist_dest, hist_user=hist_user, candidates=candidates, cand_user=cand_user, w_qu=w_qu, w_kv=w_kv, w_out=w_out)


def reference(history, hist_dest, hist_user, candidates, cand_user, w_qu, w_kv, w_out):
    head_width = D // HEAD_TOTAL
    scale = head_width ** (-0.5)
    pairs = jax.nn.silu(jnp.dot(history, w_kv, preferred_element_type=jnp.float32)).astype(jnp.bfloat16)
    qu_all = jax.nn.silu(jnp.dot(candidates, w_qu, preferred_element_type=jnp.float32)).astype(jnp.bfloat16)
    dest = hist_dest[:, 0].astype(jnp.int32)
    order = jnp.argsort(dest, stable=True).astype(jnp.int32)
    counts = lax.optimization_barrier(jnp.sum((dest[:, None] == jnp.arange(N_DP, dtype=jnp.int32)[None, :]).astype(jnp.int32), axis=0))
    starts = jnp.cumsum(counts) - counts
    group_slots = 2 * TOK_H * N_SEQ
    group_candidate_rows = C_DEV * N_SEQ

    def one_group(group):
        position = jnp.arange(group_slots, dtype=jnp.int32)
        live = position < counts[group]
        index = order[jnp.minimum(starts[group] + position, HIST - 1)]
        chosen = pairs[index]
        users = jnp.where(live, hist_user[index], -1)
        query_matrix = lax.dynamic_slice_in_dim(qu_all, (group * group_candidate_rows).astype(jnp.int32), group_candidate_rows, 0)[:, :D]
        owners = lax.dynamic_slice_in_dim(cand_user, (group * group_candidate_rows).astype(jnp.int32), group_candidate_rows, 0)
        key_rows = chosen[:, :D].reshape(group_slots, HEAD_TOTAL, head_width).astype(jnp.float32)
        value_rows = chosen[:, D:].reshape(group_slots, HEAD_TOTAL, head_width).astype(jnp.float32)
        score_matrix = jnp.einsum('clw,vlw->lcv', query_matrix.reshape(group_candidate_rows, HEAD_TOTAL, head_width).astype(jnp.float32), key_rows)
        visible = (owners[:, None] == users[None, :]).astype(jnp.float32)
        weight_matrix = (jax.nn.silu(score_matrix * scale) * visible[None]).astype(jnp.bfloat16)
        attended_values = jnp.einsum('nko,onc->knc', weight_matrix.astype(jnp.float32), value_rows)
        return attended_values.reshape(group_candidate_rows, D)
    attended_values = lax.map(one_group, jnp.arange(N_DP, dtype=jnp.int32)).reshape(CAND, D)
    mean = lax.optimization_barrier(jnp.mean(attended_values, axis=1, keepdims=True))
    centered = attended_values - mean
    variance = lax.optimization_barrier(jnp.mean(centered * centered, axis=1, keepdims=True))
    normed = centered * lax.rsqrt(variance + 1e-06)
    gated = (normed * qu_all[:, D:].astype(jnp.float32)).astype(jnp.bfloat16)
    mixed = candidates.astype(jnp.float32) + jnp.dot(gated, w_out, preferred_element_type=jnp.float32)
    return mixed
```

```python
import functools

import jax
import jax.numpy as jnp
from jax import lax
from jax.experimental import pallas as pl
from jax.experimental.pallas import tpu as pltpu
from jax.sharding import PartitionSpec as P

D = 1024
HEADS = 8
HW = D // HEADS
ROWS = 1024
GROUPS = 32
SEQ = 8
CAP = 2 * ROWS // GROUPS
CAND = 32
GROUP_CAND = CAND * SEQ
PER = 4
BATCH = PER * CAP
BATCHES = GROUPS // PER
SELF_BATCH = 2
MESH = pl.DeviceIdType.MESH
HEAD_UNROLL = 2


def silu_half(half):
    return half + half * jnp.tanh(half)


def kernel(
    history, dest_ref, user_ref, candidates, cand_user, w_qu, w_kv, w_out, out_ref,
    hist, qu_w, kv_w, out_w, send, recv, tag_send, tag_recv, slot_ref, qu, q_all, user_mat,
    mask, total, part_send, part_recv,
    load_sem, kv_sem, send_sem, recv_sem, tag_send_sem, tag_recv_sem, q_send_sem, q_recv_sem,
    part_send_sem, part_recv_sem, self_sem,
):
    dp = lax.axis_index("dp")
    z = lax.axis_index("seq")
    core = lax.rem(dp, 2)
    y = lax.rem(lax.div(dp, 2), 4)
    x = lax.div(dp, 8)
    sign = 1 - 2 * core

    load_hist = pltpu.make_async_copy(history, hist, load_sem.at[0])
    load_qu = pltpu.make_async_copy(w_qu, qu_w, load_sem.at[1])
    load_out = pltpu.make_async_copy(w_out, out_w, load_sem.at[2])
    load_hist.start()

    barrier = pltpu.get_barrier_semaphore()

    def greet(i, carry):
        @pl.when(i != dp)
        def _():
            pl.semaphore_signal(barrier, inc=1, device_id=(i, z), device_id_type=MESH)

        return carry

    lax.fori_loop(0, GROUPS, greet, 0)
    for d in range(1, SEQ):
        pl.semaphore_signal(
            barrier, inc=1, device_id=(dp, lax.rem(z + d, SEQ)), device_id_type=MESH
        )

    load_qu.start()

    def kv_copies(h):
        cols = pl.ds(pl.multiple_of(h * HW, HW), HW)
        cols_v = pl.ds(pl.multiple_of(D + h * HW, HW), HW)
        return (
            pltpu.make_async_copy(w_kv.at[:, cols], kv_w.at[h, :, pl.ds(0, HW)], kv_sem.at[2 * h]),
            pltpu.make_async_copy(
                w_kv.at[:, cols_v], kv_w.at[h, :, pl.ds(HW, HW)], kv_sem.at[2 * h + 1]
            ),
        )

    def start_kv(h, carry):
        for copy in kv_copies(h):
            copy.start()
        return carry

    lax.fori_loop(0, HEADS, start_kv, 0)
    load_out.start()

    blocks = ROWS // 128
    group_ids = lax.broadcasted_iota(jnp.int32, (GROUPS, 128), 0)
    members = [
        (dest_ref[:, b * 128 : (b + 1) * 128] == group_ids).astype(jnp.float32)
        for b in range(blocks)
    ]
    upper = (
        lax.broadcasted_iota(jnp.int32, (128, 128), 0)
        <= lax.broadcasted_iota(jnp.int32, (128, 128), 1)
    ).astype(jnp.float32)
    running = jnp.dot(
        jnp.concatenate(members, axis=0).astype(jnp.bfloat16),
        upper.astype(jnp.bfloat16),
        preferred_element_type=jnp.float32,
    )
    before = jnp.zeros((GROUPS, 1), jnp.float32)
    for b in range(blocks):
        inside = running[b * GROUPS : (b + 1) * GROUPS]
        rank = jnp.sum(members[b] * (inside + (before - 1.0)), axis=0, keepdims=True)
        slot_ref[:, b * 128 : (b + 1) * 128] = (
            dest_ref[:, b * 128 : (b + 1) * 128] * CAP + rank.astype(jnp.int32)
        )
        before = before + inside[:, 127:128]

    load_hist.wait()
    pl.semaphore_wait(barrier, GROUPS - 1 + SEQ - 1)

    def target(j, i):
        jj = lax.rem(j, 4)
        other = lax.div(j, 4)
        a = jnp.where(jj == 1, 2, 1)
        b = jnp.where(jj == 3, 0, 1)
        dx, dy = ((a, b), (-b, a), (-a, -b), (b, -a))[i]
        dx = jnp.where(jj == SELF_BATCH, 2 * (i % 2), dx)
        dy = jnp.where(jj == SELF_BATCH, 2 * (i // 2), dy)
        to_x = lax.rem(x + sign * dx + 4, 4)
        to_y = lax.rem(y + sign * dy + 4, 4)
        return to_x * 8 + to_y * 2 + lax.rem(core + other, 2)

    def row_copy(j, i):
        k = j * PER + i
        rows = pl.ds(pl.multiple_of(k * CAP, CAP), CAP)
        return pltpu.make_async_remote_copy(
            send.at[rows], recv.at[rows], send_sem.at[k], recv_sem.at[k],
            device_id=(target(j, i), z), device_id_type=MESH,
        )

    def tag_copy(j, i):
        k = j * PER + i
        return pltpu.make_async_remote_copy(
            tag_send.at[2 * j + i // 2], tag_recv.at[k], tag_send_sem.at[k], tag_recv_sem.at[k],
            device_id=(target(j, i), z), device_id_type=MESH,
        )

    self_rows = pl.ds(SELF_BATCH * PER * CAP, CAP)
    self_copy = pltpu.make_async_copy(send.at[self_rows], recv.at[self_rows], self_sem.at[0])
    self_tag = pltpu.make_async_copy(
        tag_send.at[2 * SELF_BATCH], tag_recv.at[SELF_BATCH * PER], self_sem.at[1]
    )

    users = user_ref[...].astype(jnp.float32).astype(jnp.bfloat16)
    users = jnp.broadcast_to(users, (16, ROWS))
    slot_row = slot_ref[...]

    def pack(j, carry):
        inside = lax.broadcasted_iota(jnp.int32, (CAP, ROWS), 0)
        picks = jnp.concatenate(
            [
                ((slot_row - target(j, i) * CAP) == inside).astype(jnp.float32)
                for i in range(PER)
            ],
            axis=0,
        ).astype(jnp.bfloat16)
        tags = lax.dot_general(
            users, picks, (((1,), (1,)), ((), ())), preferred_element_type=jnp.float32
        )
        tag_send[2 * j] = tags[0:1, 0:128]
        tag_send[2 * j + 1] = tags[0:1, 128:256]
        rows = pl.ds(pl.multiple_of(j * BATCH, BATCH), BATCH)
        for c in range(D // 256):
            send[rows, c * 256 : (c + 1) * 256] = jnp.dot(
                picks, hist[:, c * 256 : (c + 1) * 256], preferred_element_type=jnp.float32
            ).astype(jnp.bfloat16)
        for i in range(PER):
            if i == 0:
                @pl.when(j != SELF_BATCH)
                def _():
                    row_copy(j, 0).start()
                    tag_copy(j, 0).start()

                @pl.when(j == SELF_BATCH)
                def _():
                    self_copy.start()
                    self_tag.start()
            else:
                row_copy(j, i).start()
                tag_copy(j, i).start()
        return carry

    lax.fori_loop(0, BATCHES, pack, 0)

    load_qu.wait()

    def project_own(c, carry):
        cols = pl.ds(pl.multiple_of(c * 256, 256), 256)
        qu[:, cols] = silu_half(
            0.5 * jnp.dot(candidates[...], qu_w[:, cols], preferred_element_type=jnp.float32)
        ).astype(jnp.bfloat16)
        return carry

    lax.fori_loop(0, 2 * D // 256, project_own, 0)
    own_rows = pl.ds(pl.multiple_of(z * CAND, CAND), CAND)
    q_all[own_rows, :] = qu[:, :D]

    def q_copy(d):
        return pltpu.make_async_remote_copy(
            qu.at[:, pl.ds(0, D)], q_all.at[own_rows], q_send_sem.at[d], q_recv_sem.at[d],
            device_id=(dp, lax.rem(z + d, SEQ)), device_id_type=MESH,
        )

    for d in range(1, SEQ):
        q_copy(d).start()

    square = (
        lax.broadcasted_iota(jnp.int32, (GROUP_CAND, GROUP_CAND), 0)
        == lax.broadcasted_iota(jnp.int32, (GROUP_CAND, GROUP_CAND), 1)
    )
    cand_col = jnp.sum(
        jnp.where(square, cand_user[...].astype(jnp.float32), 0.0), axis=1, keepdims=True
    )
    user_mat[...] = jnp.broadcast_to(cand_col, (GROUP_CAND, BATCH))
    total[...] = jnp.zeros_like(total)

    def finish_kv(h, carry):
        for copy in kv_copies(h):
            copy.wait()
        return carry

    lax.fori_loop(0, HEADS, finish_kv, 0)
    for d in range(1, SEQ):
        q_copy(d).wait_recv()

    low = lax.broadcasted_iota(jnp.int32, (1, 128), 1) < CAP
    scale = 0.5 * HW ** (-0.5)

    def attend(j, carry):
        for i in range(PER):
            if i == 0:
                @pl.when(j != SELF_BATCH)
                def _():
                    row_copy(j, 0).wait_recv()
                    tag_copy(j, 0).wait_recv()

                @pl.when(j == SELF_BATCH)
                def _():
                    self_copy.wait()
                    self_tag.wait()
            else:
                row_copy(j, i).wait_recv()
                tag_copy(j, i).wait_recv()
        tags = jnp.concatenate(
            [
                jnp.where(low, tag_recv[j * PER], tag_recv[j * PER + 1]),
                jnp.where(low, tag_recv[j * PER + 2], tag_recv[j * PER + 3]),
            ],
            axis=1,
        )
        mask[...] = (user_mat[...] == tags).astype(jnp.float32)
        rows = pl.ds(pl.multiple_of(j * BATCH, BATCH), BATCH)

        def heads(step, carry):
            for sub in range(HEAD_UNROLL):
                h = step * HEAD_UNROLL + sub
                kv = silu_half(
                    0.5 * jnp.dot(recv[rows, :], kv_w[h], preferred_element_type=jnp.float32)
                ).astype(jnp.bfloat16)
                q_head = q_all[:, pl.ds(pl.multiple_of(h * HW, HW), HW)]
                half = scale * lax.dot_general(
                    q_head, kv[:, :HW], (((1,), (1,)), ((), ())),
                    preferred_element_type=jnp.float32,
                )
                weight = (silu_half(half) * mask[...]).astype(jnp.bfloat16)
                total[h] += jnp.dot(weight, kv[:, HW:], preferred_element_type=jnp.float32)
            return carry

        return lax.fori_loop(0, HEADS // HEAD_UNROLL, heads, carry)

    lax.fori_loop(0, BATCHES, attend, 0)

    for h in range(HEADS):
        part_send[:, h * HW : (h + 1) * HW] = total[h].astype(jnp.bfloat16)

    def part_copy(d):
        peer = lax.rem(z + d, SEQ)
        return pltpu.make_async_remote_copy(
            part_send.at[pl.ds(pl.multiple_of(peer * CAND, CAND), CAND)],
            part_recv.at[d], part_send_sem.at[d], part_recv_sem.at[d],
            device_id=(dp, peer), device_id_type=MESH,
        )

    for d in (4, 3, 5, 2, 6, 1, 7):
        part_copy(d).start()
    load_out.wait()
    attended = jnp.concatenate([total[h, own_rows, :] for h in range(HEADS)], axis=1)
    for d in (1, 7, 2, 6, 3, 5, 4):
        part_copy(d).wait_recv()
        attended = attended + part_recv[d].astype(jnp.float32)
    mean = jnp.mean(attended, axis=1, keepdims=True)
    centered = attended - mean
    variance = jnp.mean(centered * centered, axis=1, keepdims=True)
    normed = centered * lax.rsqrt(variance + 1e-06)
    gated = (normed * qu[:, D:].astype(jnp.float32)).astype(jnp.bfloat16)
    for c in range(D // 256):
        cols = slice(c * 256, (c + 1) * 256)
        out_ref[:, cols] = candidates[:, cols].astype(jnp.float32) + jnp.dot(
            gated, out_w[:, cols], preferred_element_type=jnp.float32
        )

    def drain(j, carry):
        for i in range(PER):
            if i == 0:
                @pl.when(j != SELF_BATCH)
                def _():
                    row_copy(j, 0).wait_send()
                    tag_copy(j, 0).wait_send()
            else:
                row_copy(j, i).wait_send()
                tag_copy(j, i).wait_send()
        return carry

    lax.fori_loop(0, BATCHES, drain, 0)
    for d in range(1, SEQ):
        q_copy(d).wait_send()
        part_copy(d).wait_send()


def on_device(history, hist_dest, hist_user, candidates, cand_user, w_qu, w_kv, w_out):
    vmem = pl.BlockSpec(memory_space=pltpu.VMEM)
    hbm = pl.BlockSpec(memory_space=pl.ANY)
    dma = pltpu.SemaphoreType.DMA
    bf16, f32 = jnp.bfloat16, jnp.float32
    return pl.pallas_call(
        kernel,
        out_shape=jax.ShapeDtypeStruct((CAND, D), f32),
        in_specs=[hbm, vmem, vmem, vmem, vmem, hbm, hbm, hbm],
        out_specs=vmem,
        scratch_shapes=[
            pltpu.VMEM((ROWS, D), bf16),
            pltpu.VMEM((D, 2 * D), bf16),
            pltpu.VMEM((HEADS, D, 2 * HW), bf16),
            pltpu.VMEM((D, D), bf16),
            pltpu.VMEM((GROUPS * CAP, D), bf16),
            pltpu.VMEM((GROUPS * CAP, D), bf16),
            pltpu.VMEM((2 * BATCHES, 1, 128), f32),
            pltpu.VMEM((GROUPS, 1, 128), f32),
            pltpu.VMEM((1, ROWS), jnp.int32),
            pltpu.VMEM((CAND, 2 * D), bf16),
            pltpu.VMEM((GROUP_CAND, D), bf16),
            pltpu.VMEM((GROUP_CAND, BATCH), f32),
            pltpu.VMEM((GROUP_CAND, BATCH), f32),
            pltpu.VMEM((HEADS, GROUP_CAND, HW), f32),
            pltpu.VMEM((GROUP_CAND, D), bf16),
            pltpu.VMEM((SEQ, CAND, D), bf16),
            dma((3,)),
            dma((2 * HEADS,)),
            dma((GROUPS,)),
            dma((GROUPS,)),
            dma((GROUPS,)),
            dma((GROUPS,)),
            dma((SEQ,)),
            dma((SEQ,)),
            dma((SEQ,)),
            dma((SEQ,)),
            dma((2,)),
        ],
        compiler_params=pltpu.CompilerParams(
            collective_id=0, has_side_effects=True, vmem_limit_bytes=56 << 20
        ),
        name="route_attend_score",
    )(
        history, hist_dest.reshape(1, ROWS), hist_user.reshape(1, ROWS), candidates,
        cand_user.reshape(1, GROUP_CAND), w_qu, w_kv, w_out,
    )


def solution(mesh):
    placed = (
        P(("dp", "seq"), None),
        P(("dp", "seq"), None),
        P(("dp", "seq")),
        P(("dp", "seq"), None),
        P("dp"),
        P(),
        P(),
        P(),
    )
    return jax.shard_map(
        on_device, mesh=mesh, in_specs=placed, out_specs=P(("dp", "seq"), None), check_vma=False
    )
```

```python
import functools

import jax
import jax.numpy as jnp
from jax import lax
from jax.experimental import pallas as pl
from jax.experimental.pallas import tpu as pltpu
from jax.sharding import PartitionSpec as P

D = 1024
HEADS = 8
HW = D // HEADS
ROWS = 1024
GROUPS = 32
SEQ = 8
CAP = 2 * ROWS // GROUPS
CAND = 32
GROUP_CAND = CAND * SEQ
PER = 4
BATCH = PER * CAP
BATCHES = GROUPS // PER
MESH = pl.DeviceIdType.MESH
PACKED_FIRST = 2
SELF_PLACE = 3


def silu_half(half):
    return half + half * jnp.tanh(half)


def kernel(
    history, dest_ref, user_ref, candidates, cand_user, w_qu, w_kv, w_out, out_ref,
    hist, qu_w, kv_w, out_w, send, recv, tag_send, tag_recv, slot_ref, qu, q_all, user_mat,
    mask, kv_ref, total, part_send, part_recv,
    load_sem, kv_sem, send_sem, recv_sem, tag_send_sem, tag_recv_sem, q_send_sem, q_recv_sem,
    part_send_sem, part_recv_sem, self_sem,
):
    dp = lax.axis_index("dp")
    z = lax.axis_index("seq")
    core = lax.rem(dp, 2)
    y = lax.rem(lax.div(dp, 2), 4)
    x = lax.div(dp, 8)
    sign = 1 - 2 * core

    step = ROWS // 4
    load_hist = [
        pltpu.make_async_copy(
            history.at[pl.ds(c * step, step)], hist.at[pl.ds(c * step, step)], load_sem.at[c]
        )
        for c in range(4)
    ]
    load_qu = pltpu.make_async_copy(w_qu, qu_w, load_sem.at[4])
    load_out = pltpu.make_async_copy(w_out, out_w, load_sem.at[5])
    for copy in load_hist:
        copy.start()

    barrier = pltpu.get_barrier_semaphore()
    for other in range(1, GROUPS):
        pl.semaphore_signal(
            barrier, inc=1, device_id=(lax.rem(dp + other, GROUPS), z), device_id_type=MESH
        )
    for d in range(1, SEQ):
        pl.semaphore_signal(
            barrier, inc=1, device_id=(dp, lax.rem(z + d, SEQ)), device_id_type=MESH
        )

    def kv_copies(h):
        cols = pl.ds(h * HW, HW)
        cols_v = pl.ds(D + h * HW, HW)
        return (
            pltpu.make_async_copy(w_kv.at[:, cols], kv_w.at[h, :, pl.ds(0, HW)], kv_sem.at[2 * h]),
            pltpu.make_async_copy(
                w_kv.at[:, cols_v], kv_w.at[h, :, pl.ds(HW, HW)], kv_sem.at[2 * h + 1]
            ),
        )

    blocks = ROWS // 128
    group_ids = lax.broadcasted_iota(jnp.int32, (GROUPS, 128), 0)
    members = [
        (dest_ref[:, b * 128 : (b + 1) * 128] == group_ids).astype(jnp.float32)
        for b in range(blocks)
    ]
    upper = (
        lax.broadcasted_iota(jnp.int32, (128, 128), 0)
        <= lax.broadcasted_iota(jnp.int32, (128, 128), 1)
    ).astype(jnp.float32)
    running = jnp.dot(
        jnp.concatenate(members, axis=0).astype(jnp.bfloat16),
        upper.astype(jnp.bfloat16),
        preferred_element_type=jnp.float32,
    )
    before = jnp.zeros((GROUPS, 1), jnp.float32)
    for b in range(blocks):
        inside = running[b * GROUPS : (b + 1) * GROUPS]
        rank = jnp.sum(members[b] * (inside + (before - 1.0)), axis=0, keepdims=True)
        slot_ref[:, b * 128 : (b + 1) * 128] = (
            dest_ref[:, b * 128 : (b + 1) * 128] * CAP + rank.astype(jnp.int32)
        )
        before = before + inside[:, 127:128]

    for copy in load_hist:
        copy.wait()
    load_qu.start()
    for h in range(HEADS):
        for copy in kv_copies(h):
            copy.start()
    load_out.start()

    def target(j, i):
        jj = lax.rem(j, 4)
        a = jnp.where(jj == 2, 2, 1)
        b = jnp.where(jj == 3, 0, 1)
        dx, dy = ((a, b), (-b, a), (-a, -b), (b, -a))[i]
        dx = jnp.where(jj == 0, 2 * (1 - i % 2), dx)
        dy = jnp.where(jj == 0, 2 * (1 - i // 2), dy)
        to_x = lax.rem(x + sign * dx + 4, 4)
        to_y = lax.rem(y + sign * dy + 4, 4)
        return to_x * 8 + to_y * 2 + lax.div(j, 4)

    def block(k):
        return pl.ds(pl.multiple_of(k * CAP, CAP), CAP)

    def row_copy(j, i):
        k = j * PER + i
        r = lax.rem(j, 4) * 2 * PER + core * PER + i
        return pltpu.make_async_remote_copy(
            send.at[block(k)], recv.at[block(r)], send_sem.at[k], recv_sem.at[r],
            device_id=(target(j, i), z), device_id_type=MESH,
        )

    def tag_copy(j, i):
        k = j * PER + i
        r = lax.rem(j, 4) * 2 * PER + core * PER + i
        return pltpu.make_async_remote_copy(
            tag_send.at[2 * j + i // 2], tag_recv.at[r], tag_send_sem.at[k], tag_recv_sem.at[r],
            device_id=(target(j, i), z), device_id_type=MESH,
        )

    def arrival(r):
        return (
            pltpu.make_async_remote_copy(
                send.at[block(r)], recv.at[block(r)], send_sem.at[r], recv_sem.at[r],
                device_id=(dp, lax.rem(z + 1, SEQ)), device_id_type=MESH,
            ),
            pltpu.make_async_remote_copy(
                tag_send.at[0], tag_recv.at[r], tag_send_sem.at[r], tag_recv_sem.at[r],
                device_id=(dp, lax.rem(z + 1, SEQ)), device_id_type=MESH,
            ),
        )

    self_part = core * 4
    self_copy = pltpu.make_async_copy(
        send.at[block(self_part * PER + SELF_PLACE)], recv.at[block(core * PER + SELF_PLACE)],
        self_sem.at[0],
    )
    self_tag = pltpu.make_async_copy(
        tag_send.at[2 * self_part + SELF_PLACE // 2], tag_recv.at[core * PER + SELF_PLACE],
        self_sem.at[1],
    )

    users = user_ref[...].astype(jnp.float32).astype(jnp.bfloat16)
    users = jnp.broadcast_to(users, (16, ROWS))
    slot_row = slot_ref[...]

    def pack(j):
        inside = lax.broadcasted_iota(jnp.int32, (CAP, ROWS), 0)
        picks = jnp.concatenate(
            [
                ((slot_row - target(j, i) * CAP) == inside).astype(jnp.float32)
                for i in range(PER)
            ],
            axis=0,
        ).astype(jnp.bfloat16)
        tags = lax.dot_general(
            users, picks, (((1,), (1,)), ((), ())), preferred_element_type=jnp.float32
        )
        tag_send[2 * j] = tags[0:1, 0:128]
        tag_send[2 * j + 1] = tags[0:1, 128:256]
        rows = pl.ds(pl.multiple_of(j * BATCH, BATCH), BATCH)
        for c in range(D // 256):
            send[rows, c * 256 : (c + 1) * 256] = jnp.dot(
                picks, hist[:, c * 256 : (c + 1) * 256], preferred_element_type=jnp.float32
            ).astype(jnp.bfloat16)

    def dispatch(j):
        for i in range(PER):
            if i == SELF_PLACE:
                @pl.when(j != self_part)
                def _():
                    row_copy(j, i).start()
                    tag_copy(j, i).start()

                @pl.when(j == self_part)
                def _():
                    self_copy.start()
                    self_tag.start()
            else:
                row_copy(j, i).start()
                tag_copy(j, i).start()

    def dispatch_and_pack(j, carry):
        dispatch(j)
        pack(j + 1)
        return carry

    pack(0)
    pl.semaphore_wait(barrier, GROUPS - 1 + SEQ - 1)
    lax.fori_loop(0, PACKED_FIRST, dispatch_and_pack, 0)

    load_qu.wait()

    for c in range(2 * D // 256):
        cols = slice(c * 256, (c + 1) * 256)
        qu[:, cols] = silu_half(
            0.5 * jnp.dot(candidates[...], qu_w[:, cols], preferred_element_type=jnp.float32)
        ).astype(jnp.bfloat16)
    own_rows = pl.ds(pl.multiple_of(z * CAND, CAND), CAND)
    q_all[own_rows, :] = qu[:, :D]

    def q_copy(d):
        return pltpu.make_async_remote_copy(
            qu.at[:, pl.ds(0, D)], q_all.at[own_rows], q_send_sem.at[d], q_recv_sem.at[d],
            device_id=(dp, lax.rem(z + d, SEQ)), device_id_type=MESH,
        )

    for d in range(1, SEQ):
        q_copy(d).start()
    lax.fori_loop(PACKED_FIRST, BATCHES - 1, dispatch_and_pack, 0)
    dispatch(BATCHES - 1)

    square = (
        lax.broadcasted_iota(jnp.int32, (GROUP_CAND, GROUP_CAND), 0)
        == lax.broadcasted_iota(jnp.int32, (GROUP_CAND, GROUP_CAND), 1)
    )
    cand_col = jnp.sum(
        jnp.where(square, cand_user[...].astype(jnp.float32), 0.0), axis=1, keepdims=True
    )
    user_mat[...] = jnp.broadcast_to(cand_col, (GROUP_CAND, BATCH))
    total[...] = jnp.zeros_like(total)

    for h in range(HEADS):
        for copy in kv_copies(h):
            copy.wait()

    low = lax.broadcasted_iota(jnp.int32, (1, 128), 1) < CAP
    scale = 0.5 * HW ** (-0.5)

    def project(b):
        for i in range(PER):
            rows_in, tags_in = arrival(b * PER + i)
            if i == SELF_PLACE:
                @pl.when(b != core)
                def _():
                    rows_in.wait_recv()
                    tags_in.wait_recv()

                @pl.when(b == core)
                def _():
                    self_copy.wait()
                    self_tag.wait()
            else:
                rows_in.wait_recv()
                tags_in.wait_recv()
        tags = jnp.concatenate(
            [
                jnp.where(low, tag_recv[b * PER], tag_recv[b * PER + 1]),
                jnp.where(low, tag_recv[b * PER + 2], tag_recv[b * PER + 3]),
            ],
            axis=1,
        )
        mask[...] = (user_mat[...] == tags).astype(jnp.float32)
        rows = pl.ds(pl.multiple_of(b * BATCH, BATCH), BATCH)
        for h in range(HEADS):
            kv_ref[h] = silu_half(
                0.5 * jnp.dot(recv[rows, :], kv_w[h], preferred_element_type=jnp.float32)
            ).astype(jnp.bfloat16)

    def attend_head(h):
        half = scale * lax.dot_general(
            q_all[:, h * HW : (h + 1) * HW], kv_ref[h, :, :HW], (((1,), (1,)), ((), ())),
            preferred_element_type=jnp.float32,
        )
        weight = (silu_half(half) * mask[...]).astype(jnp.bfloat16)
        return total[h] + jnp.dot(weight, kv_ref[h, :, HW:], preferred_element_type=jnp.float32)

    def batch(b, carry):
        project(b)

        @pl.when(b == 0)
        def _():
            for d in range(1, SEQ):
                q_copy(d).wait_recv()

        for h in range(HEADS):
            total[h] = attend_head(h)
        return carry

    lax.fori_loop(0, BATCHES - 1, batch, 0)
    shift = total[0]
    for h in range(1, HEADS):
        shift = shift + total[h]
    shift = jnp.sum(shift, axis=1, keepdims=True) * (1.0 / D)
    for h in range(HEADS):
        total[h] = total[h] - shift
    project(BATCHES - 1)
    for h in range(HEADS):
        head_total = attend_head(h)
        total[h] = head_total
        part_send[:, h * HW : (h + 1) * HW] = head_total.astype(jnp.bfloat16)

    def part_copy(d):
        peer = lax.rem(z + d, SEQ)
        return pltpu.make_async_remote_copy(
            part_send.at[pl.ds(pl.multiple_of(peer * CAND, CAND), CAND)],
            part_recv.at[d], part_send_sem.at[d], part_recv_sem.at[d],
            device_id=(dp, peer), device_id_type=MESH,
        )

    for d in (4, 3, 5, 2, 6, 1, 7):
        part_copy(d).start()
    load_out.wait()
    attended = jnp.concatenate([total[h, own_rows, :] for h in range(HEADS)], axis=1)
    for d in (1, 7, 2, 6, 3, 5, 4):
        part_copy(d).wait_recv()
        attended = attended + part_recv[d].astype(jnp.float32)
    mean = jnp.mean(attended, axis=1, keepdims=True)
    centered = attended - mean
    variance = jnp.mean(centered * centered, axis=1, keepdims=True)
    normed = centered * lax.rsqrt(variance + 1e-06)
    gated = (normed * qu[:, D:].astype(jnp.float32)).astype(jnp.bfloat16)
    for c in range(D // 256):
        cols = slice(c * 256, (c + 1) * 256)
        out_ref[:, cols] = candidates[:, cols].astype(jnp.float32) + jnp.dot(
            gated, out_w[:, cols], preferred_element_type=jnp.float32
        )

    def drain(j, carry):
        for i in range(PER):
            if i == SELF_PLACE:
                @pl.when(j != self_part)
                def _():
                    row_copy(j, i).wait_send()
                    tag_copy(j, i).wait_send()
            else:
                row_copy(j, i).wait_send()
                tag_copy(j, i).wait_send()
        return carry

    lax.fori_loop(0, BATCHES, drain, 0)
    for d in range(1, SEQ):
        q_copy(d).wait_send()
        part_copy(d).wait_send()


def on_device(history, hist_dest, hist_user, candidates, cand_user, w_qu, w_kv, w_out):
    vmem = pl.BlockSpec(memory_space=pltpu.VMEM)
    hbm = pl.BlockSpec(memory_space=pl.ANY)
    dma = pltpu.SemaphoreType.DMA
    bf16, f32 = jnp.bfloat16, jnp.float32
    return pl.pallas_call(
        kernel,
        out_shape=jax.ShapeDtypeStruct((CAND, D), f32),
        in_specs=[hbm, vmem, vmem, vmem, vmem, hbm, hbm, hbm],
        out_specs=vmem,
        scratch_shapes=[
            pltpu.VMEM((ROWS, D), bf16),
            pltpu.VMEM((D, 2 * D), bf16),
            pltpu.VMEM((HEADS, D, 2 * HW), bf16),
            pltpu.VMEM((D, D), bf16),
            pltpu.VMEM((GROUPS * CAP, D), bf16),
            pltpu.VMEM((GROUPS * CAP, D), bf16),
            pltpu.VMEM((2 * BATCHES, 1, 128), f32),
            pltpu.VMEM((GROUPS, 1, 128), f32),
            pltpu.VMEM((1, ROWS), jnp.int32),
            pltpu.VMEM((CAND, 2 * D), bf16),
            pltpu.VMEM((GROUP_CAND, D), bf16),
            pltpu.VMEM((GROUP_CAND, BATCH), f32),
            pltpu.VMEM((GROUP_CAND, BATCH), f32),
            pltpu.VMEM((HEADS, BATCH, 2 * HW), bf16),
            pltpu.VMEM((HEADS, GROUP_CAND, HW), f32),
            pltpu.VMEM((GROUP_CAND, D), bf16),
            pltpu.VMEM((SEQ, CAND, D), bf16),
            dma((6,)),
            dma((2 * HEADS,)),
            dma((GROUPS,)),
            dma((GROUPS,)),
            dma((GROUPS,)),
            dma((GROUPS,)),
            dma((SEQ,)),
            dma((SEQ,)),
            dma((SEQ,)),
            dma((SEQ,)),
            dma((2,)),
        ],
        compiler_params=pltpu.CompilerParams(
            collective_id=0, has_side_effects=True, vmem_limit_bytes=56 << 20
        ),
        name="route_attend_score",
    )(
        history, hist_dest.reshape(1, ROWS), hist_user.reshape(1, ROWS), candidates,
        cand_user.reshape(1, GROUP_CAND), w_qu, w_kv, w_out,
    )


def solution(mesh):
    placed = (
        P(("dp", "seq"), None),
        P(("dp", "seq"), None),
        P(("dp", "seq")),
        P(("dp", "seq"), None),
        P("dp"),
        P(),
        P(),
        P(),
    )
    return jax.shard_map(
        on_device, mesh=mesh, in_specs=placed, out_specs=P(("dp", "seq"), None), check_vma=False
    )
```

```python
import functools

import jax
import jax.numpy as jnp
from jax import lax
from jax.experimental import pallas as pl
from jax.experimental.pallas import tpu as pltpu
from jax.sharding import PartitionSpec as P

D = 1024
HEADS = 8
HW = D // HEADS
ROWS = 1024
GROUPS = 32
SEQ = 8
CAP = 2 * ROWS // GROUPS
CAND = 32
GROUP_CAND = CAND * SEQ
PER = 4
BATCH = PER * CAP
BATCHES = GROUPS // PER
MESH = pl.DeviceIdType.MESH
PACKED_FIRST = 2
SELF_TURN = 1
SELF_PLACE = 3
LAST = 2 * BATCH
SLICE = 2
SLICES = HEADS // SLICE


def silu_half(half):
    return half + half * jnp.tanh(half)


def kernel(
    history, dest_ref, user_ref, candidates, cand_user, w_qu, w_kv, w_out, out_ref,
    hist, qu_w, kv_w, out_w, send, recv, tag_send, tag_recv, slot_ref, qu, q_all, user_mat,
    mask, kv_ref, total, part_send, part_recv,
    load_sem, kv_sem, send_sem, recv_sem, tag_send_sem, tag_recv_sem, q_send_sem, q_recv_sem,
    part_send_sem, part_recv_sem, self_sem,
):
    dp = lax.axis_index("dp")
    z = lax.axis_index("seq")
    core = lax.rem(dp, 2)
    y = lax.rem(lax.div(dp, 2), 4)
    x = lax.div(dp, 8)
    sign = 1 - 2 * core

    step = ROWS // 4
    load_hist = [
        pltpu.make_async_copy(
            history.at[pl.ds(c * step, step)], hist.at[pl.ds(c * step, step)], load_sem.at[c]
        )
        for c in range(4)
    ]
    load_qu = pltpu.make_async_copy(w_qu, qu_w, load_sem.at[4])
    load_out = pltpu.make_async_copy(w_out, out_w, load_sem.at[5])
    for copy in load_hist:
        copy.start()

    barrier = pltpu.get_barrier_semaphore()
    for other in range(1, GROUPS):
        pl.semaphore_signal(
            barrier, inc=1, device_id=(lax.rem(dp + other, GROUPS), z), device_id_type=MESH
        )
    for d in range(1, SEQ):
        pl.semaphore_signal(
            barrier, inc=1, device_id=(dp, lax.rem(z + d, SEQ)), device_id_type=MESH
        )

    def kv_copies(h):
        cols = pl.ds(h * HW, HW)
        cols_v = pl.ds(D + h * HW, HW)
        return (
            pltpu.make_async_copy(w_kv.at[:, cols], kv_w.at[h, :, pl.ds(0, HW)], kv_sem.at[2 * h]),
            pltpu.make_async_copy(
                w_kv.at[:, cols_v], kv_w.at[h, :, pl.ds(HW, HW)], kv_sem.at[2 * h + 1]
            ),
        )

    blocks = ROWS // 128
    group_ids = lax.broadcasted_iota(jnp.int32, (GROUPS, 128), 0)
    members = [
        (dest_ref[:, b * 128 : (b + 1) * 128] == group_ids).astype(jnp.float32)
        for b in range(blocks)
    ]
    upper = (
        lax.broadcasted_iota(jnp.int32, (128, 128), 0)
        <= lax.broadcasted_iota(jnp.int32, (128, 128), 1)
    ).astype(jnp.float32)
    running = jnp.dot(
        jnp.concatenate(members, axis=0).astype(jnp.bfloat16),
        upper.astype(jnp.bfloat16),
        preferred_element_type=jnp.float32,
    )
    before = jnp.zeros((GROUPS, 1), jnp.float32)
    for b in range(blocks):
        inside = running[b * GROUPS : (b + 1) * GROUPS]
        rank = jnp.sum(members[b] * (inside + (before - 1.0)), axis=0, keepdims=True)
        slot_ref[:, b * 128 : (b + 1) * 128] = (
            dest_ref[:, b * 128 : (b + 1) * 128] * CAP + rank.astype(jnp.int32)
        )
        before = before + inside[:, 127:128]

    for copy in load_hist:
        copy.wait()
    load_qu.start()
    for h in range(HEADS):
        for copy in kv_copies(h):
            copy.start()
    load_out.start()

    def target(j, i):
        jj = lax.rem(j, 4)
        a = jnp.where(jj == 0, 2, 1)
        b = jnp.where(jj == 3, 0, 1)
        dx, dy = ((a, b), (-b, a), (-a, -b), (b, -a))[i]
        dx = jnp.where(jj == SELF_TURN, 2 * (1 - i % 2), dx)
        dy = jnp.where(jj == SELF_TURN, 2 * (1 - i // 2), dy)
        to_x = lax.rem(x + sign * dx + 4, 4)
        to_y = lax.rem(y + sign * dy + 4, 4)
        return to_x * 8 + to_y * 2 + lax.div(j, 4)

    def block(k):
        return pl.ds(pl.multiple_of(k * CAP, CAP), CAP)

    def row_copy(j, i):
        k = j * PER + i
        r = lax.rem(j, 4) * 2 * PER + core * PER + i
        return pltpu.make_async_remote_copy(
            send.at[block(k)], recv.at[block(r)], send_sem.at[k], recv_sem.at[r],
            device_id=(target(j, i), z), device_id_type=MESH,
        )

    def tag_copy(j, i):
        k = j * PER + i
        r = lax.rem(j, 4) * 2 * PER + core * PER + i
        return pltpu.make_async_remote_copy(
            tag_send.at[2 * j + i // 2], tag_recv.at[r], tag_send_sem.at[k], tag_recv_sem.at[r],
            device_id=(target(j, i), z), device_id_type=MESH,
        )

    def arrival(r):
        return (
            pltpu.make_async_remote_copy(
                send.at[block(r)], recv.at[block(r)], send_sem.at[r], recv_sem.at[r],
                device_id=(dp, lax.rem(z + 1, SEQ)), device_id_type=MESH,
            ),
            pltpu.make_async_remote_copy(
                tag_send.at[0], tag_recv.at[r], tag_send_sem.at[r], tag_recv_sem.at[r],
                device_id=(dp, lax.rem(z + 1, SEQ)), device_id_type=MESH,
            ),
        )

    self_part = core * 4 + SELF_TURN
    self_batch = 2 * SELF_TURN + core
    self_copy = pltpu.make_async_copy(
        send.at[block(self_part * PER + SELF_PLACE)], recv.at[block(self_batch * PER + SELF_PLACE)],
        self_sem.at[0],
    )
    self_tag = pltpu.make_async_copy(
        tag_send.at[2 * self_part + SELF_PLACE // 2], tag_recv.at[self_batch * PER + SELF_PLACE],
        self_sem.at[1],
    )

    users = user_ref[...].astype(jnp.float32).astype(jnp.bfloat16)
    users = jnp.broadcast_to(users, (16, ROWS))
    slot_row = slot_ref[...]

    def pack(j):
        inside = lax.broadcasted_iota(jnp.int32, (CAP, ROWS), 0)
        picks = jnp.concatenate(
            [
                ((slot_row - target(j, i) * CAP) == inside).astype(jnp.float32)
                for i in range(PER)
            ],
            axis=0,
        ).astype(jnp.bfloat16)
        tags = lax.dot_general(
            users, picks, (((1,), (1,)), ((), ())), preferred_element_type=jnp.float32
        )
        tag_send[2 * j] = tags[0:1, 0:128]
        tag_send[2 * j + 1] = tags[0:1, 128:256]
        rows = pl.ds(pl.multiple_of(j * BATCH, BATCH), BATCH)
        for c in range(D // 256):
            send[rows, c * 256 : (c + 1) * 256] = jnp.dot(
                picks, hist[:, c * 256 : (c + 1) * 256], preferred_element_type=jnp.float32
            ).astype(jnp.bfloat16)

    def dispatch(j):
        for i in range(PER):
            if i == SELF_PLACE:
                @pl.when(j != self_part)
                def _():
                    row_copy(j, i).start()
                    tag_copy(j, i).start()

                @pl.when(j == self_part)
                def _():
                    self_copy.start()
                    self_tag.start()
            else:
                row_copy(j, i).start()
                tag_copy(j, i).start()

    def dispatch_and_pack(j, carry):
        dispatch(j)
        pack(j + 1)
        return carry

    pack(0)
    pl.semaphore_wait(barrier, GROUPS - 1 + SEQ - 1)
    lax.fori_loop(0, PACKED_FIRST, dispatch_and_pack, 0)

    load_qu.wait()

    for c in range(2 * D // 256):
        cols = slice(c * 256, (c + 1) * 256)
        qu[:, cols] = silu_half(
            0.5 * jnp.dot(candidates[...], qu_w[:, cols], preferred_element_type=jnp.float32)
        ).astype(jnp.bfloat16)
    own_rows = pl.ds(pl.multiple_of(z * CAND, CAND), CAND)
    q_all[own_rows, :] = qu[:, :D]

    def q_copy(d):
        return pltpu.make_async_remote_copy(
            qu.at[:, pl.ds(0, D)], q_all.at[own_rows], q_send_sem.at[d], q_recv_sem.at[d],
            device_id=(dp, lax.rem(z + d, SEQ)), device_id_type=MESH,
        )

    for d in range(1, SEQ):
        q_copy(d).start()
    lax.fori_loop(PACKED_FIRST, BATCHES - 1, dispatch_and_pack, 0)
    dispatch(BATCHES - 1)

    square = (
        lax.broadcasted_iota(jnp.int32, (GROUP_CAND, GROUP_CAND), 0)
        == lax.broadcasted_iota(jnp.int32, (GROUP_CAND, GROUP_CAND), 1)
    )
    cand_col = jnp.sum(
        jnp.where(square, cand_user[...].astype(jnp.float32), 0.0), axis=1, keepdims=True
    )
    user_mat[...] = jnp.broadcast_to(cand_col, (GROUP_CAND, BATCH))
    total[...] = jnp.zeros_like(total)

    for h in range(HEADS):
        for copy in kv_copies(h):
            copy.wait()

    low = lax.broadcasted_iota(jnp.int32, (1, 128), 1) < CAP
    scale = 0.5 * HW ** (-0.5)

    def take_in(b, half):
        for i in range(PER):
            rows_in, tags_in = arrival(b * PER + i)
            if i == SELF_PLACE:
                @pl.when(b != self_batch)
                def _():
                    rows_in.wait_recv()
                    tags_in.wait_recv()

                @pl.when(b == self_batch)
                def _():
                    self_copy.wait()
                    self_tag.wait()
            else:
                rows_in.wait_recv()
                tags_in.wait_recv()
        tags = jnp.concatenate(
            [
                jnp.where(low, tag_recv[b * PER], tag_recv[b * PER + 1]),
                jnp.where(low, tag_recv[b * PER + 2], tag_recv[b * PER + 3]),
            ],
            axis=1,
        )
        mask[:, half * BATCH : (half + 1) * BATCH] = (user_mat[...] == tags).astype(jnp.float32)

    def project_head(h, first, count):
        rows = pl.ds(pl.multiple_of(first, BATCH), count)
        kv_ref[h, :count] = silu_half(
            0.5 * jnp.dot(recv[rows, :], kv_w[h], preferred_element_type=jnp.float32)
        ).astype(jnp.bfloat16)

    def attend_head(h, count):
        half = scale * lax.dot_general(
            q_all[:, h * HW : (h + 1) * HW], kv_ref[h, :count, :HW], (((1,), (1,)), ((), ())),
            preferred_element_type=jnp.float32,
        )
        weight = (silu_half(half) * mask[:, :count]).astype(jnp.bfloat16)
        return total[h] + jnp.dot(
            weight, kv_ref[h, :count, HW:], preferred_element_type=jnp.float32
        )

    def batch(b, carry):
        take_in(b, 0)
        for h in range(HEADS):
            project_head(h, b * BATCH, BATCH)

        @pl.when(b == 0)
        def _():
            for d in range(1, SEQ):
                q_copy(d).wait_recv()

        for h in range(HEADS):
            total[h] = attend_head(h, BATCH)
        return carry

    lax.fori_loop(0, BATCHES - 2, batch, 0)
    shift = total[0]
    for h in range(1, HEADS):
        shift = shift + total[h]
    shift = jnp.sum(shift, axis=1, keepdims=True) * (1.0 / D)
    for h in range(HEADS):
        total[h] = total[h] - shift

    def part_copy(d, n):
        peer = lax.rem(z + d, SEQ)
        cols = pl.ds(n * SLICE * HW, SLICE * HW)
        return pltpu.make_async_remote_copy(
            part_send.at[pl.ds(pl.multiple_of(peer * CAND, CAND), CAND), cols],
            part_recv.at[d, :, cols],
            part_send_sem.at[n * SEQ + d], part_recv_sem.at[n * SEQ + d],
            device_id=(dp, peer), device_id_type=MESH,
        )

    take_in(BATCHES - 2, 0)
    take_in(BATCHES - 1, 1)
    for n in range(SLICES + 1):
        for h in range(n * SLICE, min((n + 1) * SLICE, HEADS)):
            project_head(h, GROUPS * CAP - LAST, LAST)
        if n:
            for h in range((n - 1) * SLICE, n * SLICE):
                head_total = attend_head(h, LAST)
                total[h] = head_total
                part_send[:, h * HW : (h + 1) * HW] = head_total.astype(jnp.bfloat16)
            for d in (4, 3, 5, 2, 6, 1, 7):
                part_copy(d, n - 1).start()

    load_out.wait()
    slices = []
    for n in range(SLICES):
        heads = range(n * SLICE, (n + 1) * SLICE)
        some = jnp.concatenate([total[h, own_rows, :] for h in heads], axis=1)
        for d in (1, 7, 2, 6, 3, 5, 4):
            part_copy(d, n).wait_recv()
            some = some + part_recv[d, :, n * SLICE * HW : (n + 1) * SLICE * HW].astype(jnp.float32)
        slices.append(some)
    attended = jnp.concatenate(slices, axis=1)
    mean = jnp.mean(attended, axis=1, keepdims=True)
    centered = attended - mean
    variance = jnp.mean(centered * centered, axis=1, keepdims=True)
    normed = centered * lax.rsqrt(variance + 1e-06)
    gated = (normed * qu[:, D:].astype(jnp.float32)).astype(jnp.bfloat16)
    for c in range(D // 256):
        cols = slice(c * 256, (c + 1) * 256)
        out_ref[:, cols] = candidates[:, cols].astype(jnp.float32) + jnp.dot(
            gated, out_w[:, cols], preferred_element_type=jnp.float32
        )

    def drain(j, carry):
        for i in range(PER):
            if i == SELF_PLACE:
                @pl.when(j != self_part)
                def _():
                    row_copy(j, i).wait_send()
                    tag_copy(j, i).wait_send()
            else:
                row_copy(j, i).wait_send()
                tag_copy(j, i).wait_send()
        return carry

    lax.fori_loop(0, BATCHES, drain, 0)
    for d in range(1, SEQ):
        q_copy(d).wait_send()
        for n in range(SLICES):
            part_copy(d, n).wait_send()


def on_device(history, hist_dest, hist_user, candidates, cand_user, w_qu, w_kv, w_out):
    vmem = pl.BlockSpec(memory_space=pltpu.VMEM)
    hbm = pl.BlockSpec(memory_space=pl.ANY)
    dma = pltpu.SemaphoreType.DMA
    bf16, f32 = jnp.bfloat16, jnp.float32
    return pl.pallas_call(
        kernel,
        out_shape=jax.ShapeDtypeStruct((CAND, D), f32),
        in_specs=[hbm, vmem, vmem, vmem, vmem, hbm, hbm, hbm],
        out_specs=vmem,
        scratch_shapes=[
            pltpu.VMEM((ROWS, D), bf16),
            pltpu.VMEM((D, 2 * D), bf16),
            pltpu.VMEM((HEADS, D, 2 * HW), bf16),
            pltpu.VMEM((D, D), bf16),
            pltpu.VMEM((GROUPS * CAP, D), bf16),
            pltpu.VMEM((GROUPS * CAP, D), bf16),
            pltpu.VMEM((2 * BATCHES, 1, 128), f32),
            pltpu.VMEM((GROUPS, 1, 128), f32),
            pltpu.VMEM((1, ROWS), jnp.int32),
            pltpu.VMEM((CAND, 2 * D), bf16),
            pltpu.VMEM((GROUP_CAND, D), bf16),
            pltpu.VMEM((GROUP_CAND, BATCH), f32),
            pltpu.VMEM((GROUP_CAND, LAST), f32),
            pltpu.VMEM((HEADS, LAST, 2 * HW), bf16),
            pltpu.VMEM((HEADS, GROUP_CAND, HW), f32),
            pltpu.VMEM((GROUP_CAND, D), bf16),
            pltpu.VMEM((SEQ, CAND, D), bf16),
            dma((6,)),
            dma((2 * HEADS,)),
            dma((GROUPS,)),
            dma((GROUPS,)),
            dma((GROUPS,)),
            dma((GROUPS,)),
            dma((SEQ,)),
            dma((SEQ,)),
            dma((SEQ * SLICES,)),
            dma((SEQ * SLICES,)),
            dma((2,)),
        ],
        compiler_params=pltpu.CompilerParams(
            collective_id=0, has_side_effects=True, vmem_limit_bytes=56 << 20
        ),
        name="route_attend_score",
    )(
        history, hist_dest.reshape(1, ROWS), hist_user.reshape(1, ROWS), candidates,
        cand_user.reshape(1, GROUP_CAND), w_qu, w_kv, w_out,
    )


def solution(mesh):
    placed = (
        P(("dp", "seq"), None),
        P(("dp", "seq"), None),
        P(("dp", "seq")),
        P(("dp", "seq"), None),
        P("dp"),
        P(),
        P(),
        P(),
    )
    return jax.shard_map(
        on_device, mesh=mesh, in_specs=placed, out_specs=P(("dp", "seq"), None), check_vma=False
    )
```

```python
import functools

import jax
import jax.numpy as jnp
from jax import lax
from jax.experimental import pallas as pl
from jax.experimental.pallas import tpu as pltpu
from jax.sharding import PartitionSpec as P

D = 1024
HEADS = 8
HW = D // HEADS
ROWS = 1024
GROUPS = 32
SEQ = 8
CAP = 2 * ROWS // GROUPS
CAND = 32
GROUP_CAND = CAND * SEQ
PER = 4
BATCH = PER * CAP
BATCHES = GROUPS // PER
MESH = pl.DeviceIdType.MESH
PACKED_FIRST = 2
SELF_PLACE = 3
LAST = 2 * BATCH
SLICE = 2
SLICES = HEADS // SLICE


def silu_half(half):
    return half + half * jnp.tanh(half)


def kernel(
    history, dest_ref, user_ref, candidates, cand_user, w_qu, w_kv, w_out, out_ref,
    hist, qu_w, kv_w, out_w, send, recv, tag_send, tag_recv, slot_ref, qu, q_all, user_mat,
    mask, kv_ref, total, part_send, part_recv,
    load_sem, kv_sem, send_sem, recv_sem, tag_send_sem, tag_recv_sem, q_send_sem, q_recv_sem,
    part_send_sem, part_recv_sem, self_sem,
):
    dp = lax.axis_index("dp")
    z = lax.axis_index("seq")
    core = lax.rem(dp, 2)
    y = lax.rem(lax.div(dp, 2), 4)
    x = lax.div(dp, 8)
    sign = 1 - 2 * core

    step = ROWS // 4
    load_hist = [
        pltpu.make_async_copy(
            history.at[pl.ds(c * step, step)], hist.at[pl.ds(c * step, step)], load_sem.at[c]
        )
        for c in range(4)
    ]
    load_qu = pltpu.make_async_copy(w_qu, qu_w, load_sem.at[4])
    load_out = pltpu.make_async_copy(w_out, out_w, load_sem.at[5])
    for copy in load_hist:
        copy.start()

    barrier = pltpu.get_barrier_semaphore()
    for other in range(1, GROUPS):
        pl.semaphore_signal(
            barrier, inc=1, device_id=(lax.rem(dp + other, GROUPS), z), device_id_type=MESH
        )
    for d in range(1, SEQ):
        pl.semaphore_signal(
            barrier, inc=1, device_id=(dp, lax.rem(z + d, SEQ)), device_id_type=MESH
        )

    def kv_copies(h):
        cols = pl.ds(h * HW, HW)
        cols_v = pl.ds(D + h * HW, HW)
        return (
            pltpu.make_async_copy(w_kv.at[:, cols], kv_w.at[h, :, pl.ds(0, HW)], kv_sem.at[2 * h]),
            pltpu.make_async_copy(
                w_kv.at[:, cols_v], kv_w.at[h, :, pl.ds(HW, HW)], kv_sem.at[2 * h + 1]
            ),
        )

    blocks = ROWS // 128
    group_ids = lax.broadcasted_iota(jnp.int32, (GROUPS, 128), 0)
    members = [
        (dest_ref[:, b * 128 : (b + 1) * 128] == group_ids).astype(jnp.float32)
        for b in range(blocks)
    ]
    upper = (
        lax.broadcasted_iota(jnp.int32, (128, 128), 0)
        <= lax.broadcasted_iota(jnp.int32, (128, 128), 1)
    ).astype(jnp.float32)
    running = jnp.dot(
        jnp.concatenate(members, axis=0).astype(jnp.bfloat16),
        upper.astype(jnp.bfloat16),
        preferred_element_type=jnp.float32,
    )
    before = jnp.zeros((GROUPS, 1), jnp.float32)
    for b in range(blocks):
        inside = running[b * GROUPS : (b + 1) * GROUPS]
        rank = jnp.sum(members[b] * (inside + (before - 1.0)), axis=0, keepdims=True)
        slot_ref[:, b * 128 : (b + 1) * 128] = (
            dest_ref[:, b * 128 : (b + 1) * 128] * CAP + rank.astype(jnp.int32)
        )
        before = before + inside[:, 127:128]

    for copy in load_hist:
        copy.wait()
    load_qu.start()
    for h in range(HEADS):
        for copy in kv_copies(h):
            copy.start()
    load_out.start()

    def target(j, i):
        jj = lax.rem(j, 4)
        a = jnp.where(jj == 2, 2, 1)
        b = jnp.where(jj == 3, 0, 1)
        dx, dy = ((a, b), (-b, a), (-a, -b), (b, -a))[i]
        dx = jnp.where(jj == 0, 2 * (1 - i % 2), dx)
        dy = jnp.where(jj == 0, 2 * (1 - i // 2), dy)
        to_x = lax.rem(x + sign * dx + 4, 4)
        to_y = lax.rem(y + sign * dy + 4, 4)
        return to_x * 8 + to_y * 2 + lax.div(j, 4)

    def block(k):
        return pl.ds(pl.multiple_of(k * CAP, CAP), CAP)

    def row_copy(j, i):
        k = j * PER + i
        r = lax.rem(j, 4) * 2 * PER + core * PER + i
        return pltpu.make_async_remote_copy(
            send.at[block(k)], recv.at[block(r)], send_sem.at[k], recv_sem.at[r],
            device_id=(target(j, i), z), device_id_type=MESH,
        )

    def tag_copy(j, i):
        k = j * PER + i
        r = lax.rem(j, 4) * 2 * PER + core * PER + i
        return pltpu.make_async_remote_copy(
            tag_send.at[2 * j + i // 2], tag_recv.at[r], tag_send_sem.at[k], tag_recv_sem.at[r],
            device_id=(target(j, i), z), device_id_type=MESH,
        )

    def arrival(r):
        return (
            pltpu.make_async_remote_copy(
                send.at[block(r)], recv.at[block(r)], send_sem.at[r], recv_sem.at[r],
                device_id=(dp, lax.rem(z + 1, SEQ)), device_id_type=MESH,
            ),
            pltpu.make_async_remote_copy(
                tag_send.at[0], tag_recv.at[r], tag_send_sem.at[r], tag_recv_sem.at[r],
                device_id=(dp, lax.rem(z + 1, SEQ)), device_id_type=MESH,
            ),
        )

    self_part = core * 4
    self_copy = pltpu.make_async_copy(
        send.at[block(self_part * PER + SELF_PLACE)], recv.at[block(core * PER + SELF_PLACE)],
        self_sem.at[0],
    )
    self_tag = pltpu.make_async_copy(
        tag_send.at[2 * self_part + SELF_PLACE // 2], tag_recv.at[core * PER + SELF_PLACE],
        self_sem.at[1],
    )

    users = user_ref[...].astype(jnp.float32).astype(jnp.bfloat16)
    users = jnp.broadcast_to(users, (16, ROWS))
    slot_row = slot_ref[...]

    def pack(j):
        inside = lax.broadcasted_iota(jnp.int32, (CAP, ROWS), 0)
        picks = jnp.concatenate(
            [
                ((slot_row - target(j, i) * CAP) == inside).astype(jnp.float32)
                for i in range(PER)
            ],
            axis=0,
        ).astype(jnp.bfloat16)
        tags = lax.dot_general(
            users, picks, (((1,), (1,)), ((), ())), preferred_element_type=jnp.float32
        )
        tag_send[2 * j] = tags[0:1, 0:128]
        tag_send[2 * j + 1] = tags[0:1, 128:256]
        rows = pl.ds(pl.multiple_of(j * BATCH, BATCH), BATCH)
        for c in range(D // 256):
            send[rows, c * 256 : (c + 1) * 256] = jnp.dot(
                picks, hist[:, c * 256 : (c + 1) * 256], preferred_element_type=jnp.float32
            ).astype(jnp.bfloat16)

    def dispatch(j):
        for i in range(PER):
            if i == SELF_PLACE:
                @pl.when(j != self_part)
                def _():
                    row_copy(j, i).start()
                    tag_copy(j, i).start()

                @pl.when(j == self_part)
                def _():
                    self_copy.start()
                    self_tag.start()
            else:
                row_copy(j, i).start()
                tag_copy(j, i).start()

    def dispatch_and_pack(j, carry):
        dispatch(j)
        pack(j + 1)
        return carry

    pack(0)
    pl.semaphore_wait(barrier, GROUPS - 1 + SEQ - 1)
    lax.fori_loop(0, PACKED_FIRST, dispatch_and_pack, 0)

    load_qu.wait()

    for c in range(2 * D // 256):
        cols = slice(c * 256, (c + 1) * 256)
        qu[:, cols] = silu_half(
            0.5 * jnp.dot(candidates[...], qu_w[:, cols], preferred_element_type=jnp.float32)
        ).astype(jnp.bfloat16)
    own_rows = pl.ds(pl.multiple_of(z * CAND, CAND), CAND)
    q_all[own_rows, :] = qu[:, :D]

    def q_copy(d):
        return pltpu.make_async_remote_copy(
            qu.at[:, pl.ds(0, D)], q_all.at[own_rows], q_send_sem.at[d], q_recv_sem.at[d],
            device_id=(dp, lax.rem(z + d, SEQ)), device_id_type=MESH,
        )

    for d in range(1, SEQ):
        q_copy(d).start()
    lax.fori_loop(PACKED_FIRST, BATCHES - 1, dispatch_and_pack, 0)
    dispatch(BATCHES - 1)

    square = (
        lax.broadcasted_iota(jnp.int32, (GROUP_CAND, GROUP_CAND), 0)
        == lax.broadcasted_iota(jnp.int32, (GROUP_CAND, GROUP_CAND), 1)
    )
    cand_col = jnp.sum(
        jnp.where(square, cand_user[...].astype(jnp.float32), 0.0), axis=1, keepdims=True
    )
    user_mat[...] = jnp.broadcast_to(cand_col, (GROUP_CAND, BATCH))
    total[...] = jnp.zeros_like(total)

    for h in range(HEADS):
        for copy in kv_copies(h):
            copy.wait()

    low = lax.broadcasted_iota(jnp.int32, (1, 128), 1) < CAP
    scale = 0.5 * HW ** (-0.5)

    def take_in(b, half):
        for i in range(PER):
            rows_in, tags_in = arrival(b * PER + i)
            if i == SELF_PLACE:
                @pl.when(b != core)
                def _():
                    rows_in.wait_recv()
                    tags_in.wait_recv()

                @pl.when(b == core)
                def _():
                    self_copy.wait()
                    self_tag.wait()
            else:
                rows_in.wait_recv()
                tags_in.wait_recv()
        tags = jnp.concatenate(
            [
                jnp.where(low, tag_recv[b * PER], tag_recv[b * PER + 1]),
                jnp.where(low, tag_recv[b * PER + 2], tag_recv[b * PER + 3]),
            ],
            axis=1,
        )
        mask[:, half * BATCH : (half + 1) * BATCH] = (user_mat[...] == tags).astype(jnp.float32)

    def project_head(h, first, count):
        rows = pl.ds(pl.multiple_of(first, BATCH), count)
        kv_ref[h, :count] = silu_half(
            0.5 * jnp.dot(recv[rows, :], kv_w[h], preferred_element_type=jnp.float32)
        ).astype(jnp.bfloat16)

    def attend_head(h, count):
        half = scale * lax.dot_general(
            q_all[:, h * HW : (h + 1) * HW], kv_ref[h, :count, :HW], (((1,), (1,)), ((), ())),
            preferred_element_type=jnp.float32,
        )
        weight = (silu_half(half) * mask[:, :count]).astype(jnp.bfloat16)
        return total[h] + jnp.dot(
            weight, kv_ref[h, :count, HW:], preferred_element_type=jnp.float32
        )

    def batch(b, carry):
        take_in(b, 0)
        for h in range(HEADS):
            project_head(h, b * BATCH, BATCH)

        @pl.when(b == 0)
        def _():
            for d in range(1, SEQ):
                q_copy(d).wait_recv()

        for h in range(HEADS):
            total[h] = attend_head(h, BATCH)
        return carry

    lax.fori_loop(0, BATCHES - 2, batch, 0)
    shift = total[0]
    for h in range(1, HEADS):
        shift = shift + total[h]
    shift = jnp.sum(shift, axis=1, keepdims=True) * (1.0 / D)
    for h in range(HEADS):
        total[h] = total[h] - shift

    def part_copy(d, n):
        peer = lax.rem(z + d, SEQ)
        cols = pl.ds(n * SLICE * HW, SLICE * HW)
        return pltpu.make_async_remote_copy(
            part_send.at[pl.ds(pl.multiple_of(peer * CAND, CAND), CAND), cols],
            part_recv.at[d, :, cols],
            part_send_sem.at[n * SEQ + d], part_recv_sem.at[n * SEQ + d],
            device_id=(dp, peer), device_id_type=MESH,
        )

    take_in(BATCHES - 2, 0)
    take_in(BATCHES - 1, 1)
    for n in range(SLICES + 1):
        for h in range(n * SLICE, min((n + 1) * SLICE, HEADS)):
            project_head(h, GROUPS * CAP - LAST, LAST)
        if n:
            for h in range((n - 1) * SLICE, n * SLICE):
                head_total = attend_head(h, LAST)
                total[h] = head_total
                part_send[:, h * HW : (h + 1) * HW] = head_total.astype(jnp.bfloat16)
            for d in (4, 3, 5, 2, 6, 1, 7):
                part_copy(d, n - 1).start()

    load_out.wait()
    slices = []
    for n in range(SLICES):
        heads = range(n * SLICE, (n + 1) * SLICE)
        some = jnp.concatenate([total[h, own_rows, :] for h in heads], axis=1)
        for d in (1, 7, 2, 6, 3, 5, 4):
            part_copy(d, n).wait_recv()
            some = some + part_recv[d, :, n * SLICE * HW : (n + 1) * SLICE * HW].astype(jnp.float32)
        slices.append(some)
    attended = jnp.concatenate(slices, axis=1)
    mean = jnp.mean(attended, axis=1, keepdims=True)
    centered = attended - mean
    variance = jnp.mean(centered * centered, axis=1, keepdims=True)
    normed = centered * lax.rsqrt(variance + 1e-06)
    gated = (normed * qu[:, D:].astype(jnp.float32)).astype(jnp.bfloat16)
    for c in range(D // 256):
        cols = slice(c * 256, (c + 1) * 256)
        out_ref[:, cols] = candidates[:, cols].astype(jnp.float32) + jnp.dot(
            gated, out_w[:, cols], preferred_element_type=jnp.float32
        )

    def drain(j, carry):
        for i in range(PER):
            if i == SELF_PLACE:
                @pl.when(j != self_part)
                def _():
                    row_copy(j, i).wait_send()
                    tag_copy(j, i).wait_send()
            else:
                row_copy(j, i).wait_send()
                tag_copy(j, i).wait_send()
        return carry

    lax.fori_loop(0, BATCHES, drain, 0)
    for d in range(1, SEQ):
        q_copy(d).wait_send()
        for n in range(SLICES):
            part_copy(d, n).wait_send()


def on_device(history, hist_dest, hist_user, candidates, cand_user, w_qu, w_kv, w_out):
    vmem = pl.BlockSpec(memory_space=pltpu.VMEM)
    hbm = pl.BlockSpec(memory_space=pl.ANY)
    dma = pltpu.SemaphoreType.DMA
    bf16, f32 = jnp.bfloat16, jnp.float32
    return pl.pallas_call(
        kernel,
        out_shape=jax.ShapeDtypeStruct((CAND, D), f32),
        in_specs=[hbm, vmem, vmem, vmem, vmem, hbm, hbm, hbm],
        out_specs=vmem,
        scratch_shapes=[
            pltpu.VMEM((ROWS, D), bf16),
            pltpu.VMEM((D, 2 * D), bf16),
            pltpu.VMEM((HEADS, D, 2 * HW), bf16),
            pltpu.VMEM((D, D), bf16),
            pltpu.VMEM((GROUPS * CAP, D), bf16),
            pltpu.VMEM((GROUPS * CAP, D), bf16),
            pltpu.VMEM((2 * BATCHES, 1, 128), f32),
            pltpu.VMEM((GROUPS, 1, 128), f32),
            pltpu.VMEM((1, ROWS), jnp.int32),
            pltpu.VMEM((CAND, 2 * D), bf16),
            pltpu.VMEM((GROUP_CAND, D), bf16),
            pltpu.VMEM((GROUP_CAND, BATCH), f32),
            pltpu.VMEM((GROUP_CAND, LAST), f32),
            pltpu.VMEM((HEADS, LAST, 2 * HW), bf16),
            pltpu.VMEM((HEADS, GROUP_CAND, HW), f32),
            pltpu.VMEM((GROUP_CAND, D), bf16),
            pltpu.VMEM((SEQ, CAND, D), bf16),
            dma((6,)),
            dma((2 * HEADS,)),
            dma((GROUPS,)),
            dma((GROUPS,)),
            dma((GROUPS,)),
            dma((GROUPS,)),
            dma((SEQ,)),
            dma((SEQ,)),
            dma((SEQ * SLICES,)),
            dma((SEQ * SLICES,)),
            dma((2,)),
        ],
        compiler_params=pltpu.CompilerParams(
            collective_id=0, has_side_effects=True, vmem_limit_bytes=56 << 20
        ),
        name="route_attend_score",
    )(
        history, hist_dest.reshape(1, ROWS), hist_user.reshape(1, ROWS), candidates,
        cand_user.reshape(1, GROUP_CAND), w_qu, w_kv, w_out,
    )


def solution(mesh):
    placed = (
        P(("dp", "seq"), None),
        P(("dp", "seq"), None),
        P(("dp", "seq")),
        P(("dp", "seq"), None),
        P("dp"),
        P(),
        P(),
        P(),
    )
    return jax.shard_map(
        on_device, mesh=mesh, in_specs=placed, out_specs=P(("dp", "seq"), None), check_vma=False
    )
```

```python
import functools

import jax
import jax.numpy as jnp
from jax import lax
from jax.experimental import pallas as pl
from jax.experimental.pallas import tpu as pltpu
from jax.sharding import PartitionSpec as P

D = 1024
HEADS = 8
HW = D // HEADS
ROWS = 1024
GROUPS = 32
SEQ = 8
CAP = 2 * ROWS // GROUPS
CAND = 32
GROUP_CAND = CAND * SEQ
PER = 4
BATCH = PER * CAP
BATCHES = GROUPS // PER
MESH = pl.DeviceIdType.MESH
PACKED_FIRST = 2
SELF_PLACE = 3
LAST = 2 * BATCH
SLICE = 2
SLICES = HEADS // SLICE


def silu_half(half):
    return half + half * jnp.tanh(half)


def kernel(
    history, dest_ref, user_ref, candidates, cand_user, w_qu, w_kv, w_out, out_ref,
    hist, qu_w, kv_w, out_w, send, recv, tag_send, tag_recv, slot_ref, qu, q_all, user_mat,
    mask, kv_ref, total, part_send, part_recv,
    load_sem, kv_sem, send_sem, recv_sem, tag_send_sem, tag_recv_sem, q_send_sem, q_recv_sem,
    part_send_sem, part_recv_sem, self_sem,
):
    dp = lax.axis_index("dp")
    z = lax.axis_index("seq")
    core = lax.rem(dp, 2)
    y = lax.rem(lax.div(dp, 2), 4)
    x = lax.div(dp, 8)
    sign = 1 - 2 * core

    step = ROWS // 4
    load_hist = [
        pltpu.make_async_copy(
            history.at[pl.ds(c * step, step)], hist.at[pl.ds(c * step, step)], load_sem.at[c]
        )
        for c in range(4)
    ]
    load_qu = pltpu.make_async_copy(w_qu, qu_w, load_sem.at[4])
    load_out = pltpu.make_async_copy(w_out, out_w, load_sem.at[5])
    for copy in load_hist:
        copy.start()

    barrier = pltpu.get_barrier_semaphore()
    for other in range(1, GROUPS):
        pl.semaphore_signal(
            barrier, inc=1, device_id=(lax.rem(dp + other, GROUPS), z), device_id_type=MESH
        )
    for d in range(1, SEQ):
        pl.semaphore_signal(
            barrier, inc=1, device_id=(dp, lax.rem(z + d, SEQ)), device_id_type=MESH
        )

    def kv_copies(h):
        cols = pl.ds(h * HW, HW)
        cols_v = pl.ds(D + h * HW, HW)
        return (
            pltpu.make_async_copy(w_kv.at[:, cols], kv_w.at[h, :, pl.ds(0, HW)], kv_sem.at[2 * h]),
            pltpu.make_async_copy(
                w_kv.at[:, cols_v], kv_w.at[h, :, pl.ds(HW, HW)], kv_sem.at[2 * h + 1]
            ),
        )

    blocks = ROWS // 128
    group_ids = lax.broadcasted_iota(jnp.int32, (GROUPS, 128), 0)
    members = [
        (dest_ref[:, b * 128 : (b + 1) * 128] == group_ids).astype(jnp.float32)
        for b in range(blocks)
    ]
    upper = (
        lax.broadcasted_iota(jnp.int32, (128, 128), 0)
        <= lax.broadcasted_iota(jnp.int32, (128, 128), 1)
    ).astype(jnp.float32)
    running = jnp.dot(
        jnp.concatenate(members, axis=0).astype(jnp.bfloat16),
        upper.astype(jnp.bfloat16),
        preferred_element_type=jnp.float32,
    )
    before = jnp.zeros((GROUPS, 1), jnp.float32)
    for b in range(blocks):
        inside = running[b * GROUPS : (b + 1) * GROUPS]
        rank = jnp.sum(members[b] * (inside + (before - 1.0)), axis=0, keepdims=True)
        slot_ref[:, b * 128 : (b + 1) * 128] = (
            dest_ref[:, b * 128 : (b + 1) * 128] * CAP + rank.astype(jnp.int32)
        )
        before = before + inside[:, 127:128]

    for copy in load_hist:
        copy.wait()
    load_qu.start()
    for h in range(HEADS):
        for copy in kv_copies(h):
            copy.start()
    load_out.start()

    def target(j, i):
        jj = lax.rem(j, 4)
        a = jnp.where(jj == 2, 2, 1)
        b = jnp.where(jj == 1, 0, 1)
        dx, dy = ((a, b), (-b, a), (-a, -b), (b, -a))[i]
        dx = jnp.where(jj == 0, 2 * (1 - i % 2), dx)
        dy = jnp.where(jj == 0, 2 * (1 - i // 2), dy)
        to_x = lax.rem(x + sign * dx + 4, 4)
        to_y = lax.rem(y + sign * dy + 4, 4)
        return to_x * 8 + to_y * 2 + lax.div(j, 4)

    def block(k):
        return pl.ds(pl.multiple_of(k * CAP, CAP), CAP)

    def row_copy(j, i):
        k = j * PER + i
        r = lax.rem(j, 4) * 2 * PER + core * PER + i
        return pltpu.make_async_remote_copy(
            send.at[block(k)], recv.at[block(r)], send_sem.at[k], recv_sem.at[r],
            device_id=(target(j, i), z), device_id_type=MESH,
        )

    def tag_copy(j, i):
        k = j * PER + i
        r = lax.rem(j, 4) * 2 * PER + core * PER + i
        return pltpu.make_async_remote_copy(
            tag_send.at[2 * j + i // 2], tag_recv.at[r], tag_send_sem.at[k], tag_recv_sem.at[r],
            device_id=(target(j, i), z), device_id_type=MESH,
        )

    def arrival(r):
        return (
            pltpu.make_async_remote_copy(
                send.at[block(r)], recv.at[block(r)], send_sem.at[r], recv_sem.at[r],
                device_id=(dp, lax.rem(z + 1, SEQ)), device_id_type=MESH,
            ),
            pltpu.make_async_remote_copy(
                tag_send.at[0], tag_recv.at[r], tag_send_sem.at[r], tag_recv_sem.at[r],
                device_id=(dp, lax.rem(z + 1, SEQ)), device_id_type=MESH,
            ),
        )

    self_part = core * 4
    self_copy = pltpu.make_async_copy(
        send.at[block(self_part * PER + SELF_PLACE)], recv.at[block(core * PER + SELF_PLACE)],
        self_sem.at[0],
    )
    self_tag = pltpu.make_async_copy(
        tag_send.at[2 * self_part + SELF_PLACE // 2], tag_recv.at[core * PER + SELF_PLACE],
        self_sem.at[1],
    )

    users = user_ref[...].astype(jnp.float32).astype(jnp.bfloat16)
    users = jnp.broadcast_to(users, (16, ROWS))
    slot_row = slot_ref[...]

    def pack(j):
        inside = lax.broadcasted_iota(jnp.int32, (CAP, ROWS), 0)
        picks = jnp.concatenate(
            [
                ((slot_row - target(j, i) * CAP) == inside).astype(jnp.float32)
                for i in range(PER)
            ],
            axis=0,
        ).astype(jnp.bfloat16)
        tags = lax.dot_general(
            users, picks, (((1,), (1,)), ((), ())), preferred_element_type=jnp.float32
        )
        tag_send[2 * j] = tags[0:1, 0:128]
        tag_send[2 * j + 1] = tags[0:1, 128:256]
        rows = pl.ds(pl.multiple_of(j * BATCH, BATCH), BATCH)
        for c in range(D // 256):
            send[rows, c * 256 : (c + 1) * 256] = jnp.dot(
                picks, hist[:, c * 256 : (c + 1) * 256], preferred_element_type=jnp.float32
            ).astype(jnp.bfloat16)

    def dispatch(j):
        for i in range(PER):
            if i == SELF_PLACE:
                @pl.when(j != self_part)
                def _():
                    row_copy(j, i).start()
                    tag_copy(j, i).start()

                @pl.when(j == self_part)
                def _():
                    self_copy.start()
                    self_tag.start()
            else:
                row_copy(j, i).start()
                tag_copy(j, i).start()

    def dispatch_and_pack(j, carry):
        dispatch(j)
        pack(j + 1)
        return carry

    pack(0)
    pl.semaphore_wait(barrier, GROUPS - 1 + SEQ - 1)
    lax.fori_loop(0, PACKED_FIRST, dispatch_and_pack, 0)

    load_qu.wait()

    for c in range(2 * D // 256):
        cols = slice(c * 256, (c + 1) * 256)
        qu[:, cols] = silu_half(
            0.5 * jnp.dot(candidates[...], qu_w[:, cols], preferred_element_type=jnp.float32)
        ).astype(jnp.bfloat16)
    own_rows = pl.ds(pl.multiple_of(z * CAND, CAND), CAND)
    q_all[own_rows, :] = qu[:, :D]

    def q_copy(d):
        return pltpu.make_async_remote_copy(
            qu.at[:, pl.ds(0, D)], q_all.at[own_rows], q_send_sem.at[d], q_recv_sem.at[d],
            device_id=(dp, lax.rem(z + d, SEQ)), device_id_type=MESH,
        )

    for d in range(1, SEQ):
        q_copy(d).start()
    lax.fori_loop(PACKED_FIRST, BATCHES - 1, dispatch_and_pack, 0)
    dispatch(BATCHES - 1)

    square = (
        lax.broadcasted_iota(jnp.int32, (GROUP_CAND, GROUP_CAND), 0)
        == lax.broadcasted_iota(jnp.int32, (GROUP_CAND, GROUP_CAND), 1)
    )
    cand_col = jnp.sum(
        jnp.where(square, cand_user[...].astype(jnp.float32), 0.0), axis=1, keepdims=True
    )
    user_mat[...] = jnp.broadcast_to(cand_col, (GROUP_CAND, BATCH))
    total[...] = jnp.zeros_like(total)

    for h in range(HEADS):
        for copy in kv_copies(h):
            copy.wait()

    low = lax.broadcasted_iota(jnp.int32, (1, 128), 1) < CAP
    scale = 0.5 * HW ** (-0.5)

    def take_in(b, half):
        for i in range(PER):
            rows_in, tags_in = arrival(b * PER + i)
            if i == SELF_PLACE:
                @pl.when(b != core)
                def _():
                    rows_in.wait_recv()
                    tags_in.wait_recv()

                @pl.when(b == core)
                def _():
                    self_copy.wait()
                    self_tag.wait()
            else:
                rows_in.wait_recv()
                tags_in.wait_recv()
        tags = jnp.concatenate(
            [
                jnp.where(low, tag_recv[b * PER], tag_recv[b * PER + 1]),
                jnp.where(low, tag_recv[b * PER + 2], tag_recv[b * PER + 3]),
            ],
            axis=1,
        )
        mask[:, half * BATCH : (half + 1) * BATCH] = (user_mat[...] == tags).astype(jnp.float32)

    def project_head(h, first, count):
        rows = pl.ds(pl.multiple_of(first, BATCH), count)
        kv_ref[h, :count] = silu_half(
            0.5 * jnp.dot(recv[rows, :], kv_w[h], preferred_element_type=jnp.float32)
        ).astype(jnp.bfloat16)

    def attend_head(h, count):
        half = scale * lax.dot_general(
            q_all[:, h * HW : (h + 1) * HW], kv_ref[h, :count, :HW], (((1,), (1,)), ((), ())),
            preferred_element_type=jnp.float32,
        )
        weight = (silu_half(half) * mask[:, :count]).astype(jnp.bfloat16)
        return total[h] + jnp.dot(
            weight, kv_ref[h, :count, HW:], preferred_element_type=jnp.float32
        )

    def batch(b, carry):
        take_in(b, 0)
        for h in range(HEADS):
            project_head(h, b * BATCH, BATCH)

        @pl.when(b == 0)
        def _():
            for d in range(1, SEQ):
                q_copy(d).wait_recv()

        for h in range(HEADS):
            total[h] = attend_head(h, BATCH)
        return carry

    lax.fori_loop(0, BATCHES - 2, batch, 0)
    shift = total[0]
    for h in range(1, HEADS):
        shift = shift + total[h]
    shift = jnp.sum(shift, axis=1, keepdims=True) * (1.0 / D)
    for h in range(HEADS):
        total[h] = total[h] - shift

    def part_copy(d, n):
        peer = lax.rem(z + d, SEQ)
        cols = pl.ds(n * SLICE * HW, SLICE * HW)
        return pltpu.make_async_remote_copy(
            part_send.at[pl.ds(pl.multiple_of(peer * CAND, CAND), CAND), cols],
            part_recv.at[d, :, cols],
            part_send_sem.at[n * SEQ + d], part_recv_sem.at[n * SEQ + d],
            device_id=(dp, peer), device_id_type=MESH,
        )

    take_in(BATCHES - 2, 0)
    take_in(BATCHES - 1, 1)
    for n in range(SLICES + 1):
        for h in range(n * SLICE, min((n + 1) * SLICE, HEADS)):
            project_head(h, GROUPS * CAP - LAST, LAST)
        if n:
            for h in range((n - 1) * SLICE, n * SLICE):
                head_total = attend_head(h, LAST)
                total[h] = head_total
                part_send[:, h * HW : (h + 1) * HW] = head_total.astype(jnp.bfloat16)
            for d in (4, 3, 5, 2, 6, 1, 7):
                part_copy(d, n - 1).start()

    load_out.wait()
    slices = []
    for n in range(SLICES):
        heads = range(n * SLICE, (n + 1) * SLICE)
        some = jnp.concatenate([total[h, own_rows, :] for h in heads], axis=1)
        for d in (1, 7, 2, 6, 3, 5, 4):
            part_copy(d, n).wait_recv()
            some = some + part_recv[d, :, n * SLICE * HW : (n + 1) * SLICE * HW].astype(jnp.float32)
        slices.append(some)
    attended = jnp.concatenate(slices, axis=1)
    mean = jnp.mean(attended, axis=1, keepdims=True)
    centered = attended - mean
    variance = jnp.mean(centered * centered, axis=1, keepdims=True)
    normed = centered * lax.rsqrt(variance + 1e-06)
    gated = (normed * qu[:, D:].astype(jnp.float32)).astype(jnp.bfloat16)
    for c in range(D // 256):
        cols = slice(c * 256, (c + 1) * 256)
        out_ref[:, cols] = candidates[:, cols].astype(jnp.float32) + jnp.dot(
            gated, out_w[:, cols], preferred_element_type=jnp.float32
        )

    def drain(j, carry):
        for i in range(PER):
            if i == SELF_PLACE:
                @pl.when(j != self_part)
                def _():
                    row_copy(j, i).wait_send()
                    tag_copy(j, i).wait_send()
            else:
                row_copy(j, i).wait_send()
                tag_copy(j, i).wait_send()
        return carry

    lax.fori_loop(0, BATCHES, drain, 0)
    for d in range(1, SEQ):
        q_copy(d).wait_send()
        for n in range(SLICES):
            part_copy(d, n).wait_send()


def on_device(history, hist_dest, hist_user, candidates, cand_user, w_qu, w_kv, w_out):
    vmem = pl.BlockSpec(memory_space=pltpu.VMEM)
    hbm = pl.BlockSpec(memory_space=pl.ANY)
    dma = pltpu.SemaphoreType.DMA
    bf16, f32 = jnp.bfloat16, jnp.float32
    return pl.pallas_call(
        kernel,
        out_shape=jax.ShapeDtypeStruct((CAND, D), f32),
        in_specs=[hbm, vmem, vmem, vmem, vmem, hbm, hbm, hbm],
        out_specs=vmem,
        scratch_shapes=[
            pltpu.VMEM((ROWS, D), bf16),
            pltpu.VMEM((D, 2 * D), bf16),
            pltpu.VMEM((HEADS, D, 2 * HW), bf16),
            pltpu.VMEM((D, D), bf16),
            pltpu.VMEM((GROUPS * CAP, D), bf16),
            pltpu.VMEM((GROUPS * CAP, D), bf16),
            pltpu.VMEM((2 * BATCHES, 1, 128), f32),
            pltpu.VMEM((GROUPS, 1, 128), f32),
            pltpu.VMEM((1, ROWS), jnp.int32),
            pltpu.VMEM((CAND, 2 * D), bf16),
            pltpu.VMEM((GROUP_CAND, D), bf16),
            pltpu.VMEM((GROUP_CAND, BATCH), f32),
            pltpu.VMEM((GROUP_CAND, LAST), f32),
            pltpu.VMEM((HEADS, LAST, 2 * HW), bf16),
            pltpu.VMEM((HEADS, GROUP_CAND, HW), f32),
            pltpu.VMEM((GROUP_CAND, D), bf16),
            pltpu.VMEM((SEQ, CAND, D), bf16),
            dma((6,)),
            dma((2 * HEADS,)),
            dma((GROUPS,)),
            dma((GROUPS,)),
            dma((GROUPS,)),
            dma((GROUPS,)),
            dma((SEQ,)),
            dma((SEQ,)),
            dma((SEQ * SLICES,)),
            dma((SEQ * SLICES,)),
            dma((2,)),
        ],
        compiler_params=pltpu.CompilerParams(
            collective_id=0, has_side_effects=True, vmem_limit_bytes=56 << 20
        ),
        name="route_attend_score",
    )(
        history, hist_dest.reshape(1, ROWS), hist_user.reshape(1, ROWS), candidates,
        cand_user.reshape(1, GROUP_CAND), w_qu, w_kv, w_out,
    )


def solution(mesh):
    placed = (
        P(("dp", "seq"), None),
        P(("dp", "seq"), None),
        P(("dp", "seq")),
        P(("dp", "seq"), None),
        P("dp"),
        P(),
        P(),
        P(),
    )
    return jax.shard_map(
        on_device, mesh=mesh, in_specs=placed, out_specs=P(("dp", "seq"), None), check_vma=False
    )
```

```python
import functools

import jax
import jax.numpy as jnp
from jax import lax
from jax.experimental import pallas as pl
from jax.experimental.pallas import tpu as pltpu
from jax.sharding import PartitionSpec as P

D = 1024
HEADS = 8
HW = D // HEADS
ROWS = 1024
GROUPS = 32
SEQ = 8
CAP = 2 * ROWS // GROUPS
CAND = 32
GROUP_CAND = CAND * SEQ
PER = 4
BATCH = PER * CAP
BATCHES = GROUPS // PER
MESH = pl.DeviceIdType.MESH
PACKED_FIRST = 2
SELF_PLACE = 3
LAST = 2 * BATCH
SLICE = 2
SLICES = HEADS // SLICE


def silu_half(half):
    return half + half * jnp.tanh(half)


def kernel(
    history, dest_ref, user_ref, candidates, cand_user, w_qu, w_kv, w_out, out_ref,
    hist, qu_w, kv_w, out_w, send, recv, tag_send, tag_recv, slot_ref, qu, q_all, user_mat,
    mask, kv_ref, total, part_send, part_recv,
    load_sem, kv_sem, send_sem, recv_sem, tag_send_sem, tag_recv_sem, q_send_sem, q_recv_sem,
    part_send_sem, part_recv_sem, self_sem,
):
    dp = lax.axis_index("dp")
    z = lax.axis_index("seq")
    core = lax.rem(dp, 2)
    y = lax.rem(lax.div(dp, 2), 4)
    x = lax.div(dp, 8)
    sign = 1 - 2 * core

    step = ROWS // 4
    load_hist = [
        pltpu.make_async_copy(
            history.at[pl.ds(c * step, step)], hist.at[pl.ds(c * step, step)], load_sem.at[c]
        )
        for c in range(4)
    ]
    load_qu = pltpu.make_async_copy(w_qu, qu_w, load_sem.at[4])
    load_out = pltpu.make_async_copy(w_out, out_w, load_sem.at[5])
    for copy in load_hist:
        copy.start()

    barrier = pltpu.get_barrier_semaphore()
    for other in range(1, GROUPS):
        pl.semaphore_signal(
            barrier, inc=1, device_id=(lax.rem(dp + other, GROUPS), z), device_id_type=MESH
        )
    for d in range(1, SEQ):
        pl.semaphore_signal(
            barrier, inc=1, device_id=(dp, lax.rem(z + d, SEQ)), device_id_type=MESH
        )

    def kv_copies(h):
        cols = pl.ds(h * HW, HW)
        cols_v = pl.ds(D + h * HW, HW)
        return (
            pltpu.make_async_copy(w_kv.at[:, cols], kv_w.at[h, :, pl.ds(0, HW)], kv_sem.at[2 * h]),
            pltpu.make_async_copy(
                w_kv.at[:, cols_v], kv_w.at[h, :, pl.ds(HW, HW)], kv_sem.at[2 * h + 1]
            ),
        )

    blocks = ROWS // 128
    group_ids = lax.broadcasted_iota(jnp.int32, (GROUPS, 128), 0)
    members = [
        (dest_ref[:, b * 128 : (b + 1) * 128] == group_ids).astype(jnp.float32)
        for b in range(blocks)
    ]
    upper = (
        lax.broadcasted_iota(jnp.int32, (128, 128), 0)
        <= lax.broadcasted_iota(jnp.int32, (128, 128), 1)
    ).astype(jnp.float32)
    running = jnp.dot(
        jnp.concatenate(members, axis=0).astype(jnp.bfloat16),
        upper.astype(jnp.bfloat16),
        preferred_element_type=jnp.float32,
    )
    before = jnp.zeros((GROUPS, 1), jnp.float32)
    for b in range(blocks):
        inside = running[b * GROUPS : (b + 1) * GROUPS]
        rank = jnp.sum(members[b] * (inside + (before - 1.0)), axis=0, keepdims=True)
        slot_ref[:, b * 128 : (b + 1) * 128] = (
            dest_ref[:, b * 128 : (b + 1) * 128] * CAP + rank.astype(jnp.int32)
        )
        before = before + inside[:, 127:128]

    for copy in load_hist:
        copy.wait()
    load_qu.start()
    for h in range(HEADS):
        for copy in kv_copies(h):
            copy.start()
    load_out.start()

    def target(j, i):
        jj = lax.rem(j, 4)
        a = jnp.where((j == 2) | (j == 5), 2, 1)
        b = jnp.where((j == 3) | (j == 6), 0, 1)
        dx, dy = ((a, b), (-b, a), (-a, -b), (b, -a))[i]
        dx = jnp.where(jj == 0, 2 * (1 - i % 2), dx)
        dy = jnp.where(jj == 0, 2 * (1 - i // 2), dy)
        to_x = lax.rem(x + sign * dx + 4, 4)
        to_y = lax.rem(y + sign * dy + 4, 4)
        return to_x * 8 + to_y * 2 + lax.div(j, 4)

    def block(k):
        return pl.ds(pl.multiple_of(k * CAP, CAP), CAP)

    def row_copy(j, i):
        k = j * PER + i
        r = lax.rem(j, 4) * 2 * PER + core * PER + i
        return pltpu.make_async_remote_copy(
            send.at[block(k)], recv.at[block(r)], send_sem.at[k], recv_sem.at[r],
            device_id=(target(j, i), z), device_id_type=MESH,
        )

    def tag_copy(j, i):
        k = j * PER + i
        r = lax.rem(j, 4) * 2 * PER + core * PER + i
        return pltpu.make_async_remote_copy(
            tag_send.at[2 * j + i // 2], tag_recv.at[r], tag_send_sem.at[k], tag_recv_sem.at[r],
            device_id=(target(j, i), z), device_id_type=MESH,
        )

    def arrival(r):
        return (
            pltpu.make_async_remote_copy(
                send.at[block(r)], recv.at[block(r)], send_sem.at[r], recv_sem.at[r],
                device_id=(dp, lax.rem(z + 1, SEQ)), device_id_type=MESH,
            ),
            pltpu.make_async_remote_copy(
                tag_send.at[0], tag_recv.at[r], tag_send_sem.at[r], tag_recv_sem.at[r],
                device_id=(dp, lax.rem(z + 1, SEQ)), device_id_type=MESH,
            ),
        )

    self_part = core * 4
    self_copy = pltpu.make_async_copy(
        send.at[block(self_part * PER + SELF_PLACE)], recv.at[block(core * PER + SELF_PLACE)],
        self_sem.at[0],
    )
    self_tag = pltpu.make_async_copy(
        tag_send.at[2 * self_part + SELF_PLACE // 2], tag_recv.at[core * PER + SELF_PLACE],
        self_sem.at[1],
    )

    users = user_ref[...].astype(jnp.float32).astype(jnp.bfloat16)
    users = jnp.broadcast_to(users, (16, ROWS))
    slot_row = slot_ref[...]

    def pack(j):
        inside = lax.broadcasted_iota(jnp.int32, (CAP, ROWS), 0)
        picks = jnp.concatenate(
            [
                ((slot_row - target(j, i) * CAP) == inside).astype(jnp.float32)
                for i in range(PER)
            ],
            axis=0,
        ).astype(jnp.bfloat16)
        tags = lax.dot_general(
            users, picks, (((1,), (1,)), ((), ())), preferred_element_type=jnp.float32
        )
        tag_send[2 * j] = tags[0:1, 0:128]
        tag_send[2 * j + 1] = tags[0:1, 128:256]
        rows = pl.ds(pl.multiple_of(j * BATCH, BATCH), BATCH)
        for c in range(D // 256):
            send[rows, c * 256 : (c + 1) * 256] = jnp.dot(
                picks, hist[:, c * 256 : (c + 1) * 256], preferred_element_type=jnp.float32
            ).astype(jnp.bfloat16)

    def dispatch(j):
        for i in range(PER):
            if i == SELF_PLACE:
                @pl.when(j != self_part)
                def _():
                    row_copy(j, i).start()
                    tag_copy(j, i).start()

                @pl.when(j == self_part)
                def _():
                    self_copy.start()
                    self_tag.start()
            else:
                row_copy(j, i).start()
                tag_copy(j, i).start()

    def dispatch_and_pack(j, carry):
        dispatch(j)
        pack(j + 1)
        return carry

    pack(0)
    pl.semaphore_wait(barrier, GROUPS - 1 + SEQ - 1)
    lax.fori_loop(0, PACKED_FIRST, dispatch_and_pack, 0)

    load_qu.wait()

    for c in range(2 * D // 256):
        cols = slice(c * 256, (c + 1) * 256)
        qu[:, cols] = silu_half(
            0.5 * jnp.dot(candidates[...], qu_w[:, cols], preferred_element_type=jnp.float32)
        ).astype(jnp.bfloat16)
    own_rows = pl.ds(pl.multiple_of(z * CAND, CAND), CAND)
    q_all[own_rows, :] = qu[:, :D]

    def q_copy(d):
        return pltpu.make_async_remote_copy(
            qu.at[:, pl.ds(0, D)], q_all.at[own_rows], q_send_sem.at[d], q_recv_sem.at[d],
            device_id=(dp, lax.rem(z + d, SEQ)), device_id_type=MESH,
        )

    for d in range(1, SEQ):
        q_copy(d).start()
    lax.fori_loop(PACKED_FIRST, BATCHES - 1, dispatch_and_pack, 0)
    dispatch(BATCHES - 1)

    square = (
        lax.broadcasted_iota(jnp.int32, (GROUP_CAND, GROUP_CAND), 0)
        == lax.broadcasted_iota(jnp.int32, (GROUP_CAND, GROUP_CAND), 1)
    )
    cand_col = jnp.sum(
        jnp.where(square, cand_user[...].astype(jnp.float32), 0.0), axis=1, keepdims=True
    )
    user_mat[...] = jnp.broadcast_to(cand_col, (GROUP_CAND, BATCH))
    total[...] = jnp.zeros_like(total)

    for h in range(HEADS):
        for copy in kv_copies(h):
            copy.wait()

    low = lax.broadcasted_iota(jnp.int32, (1, 128), 1) < CAP
    scale = 0.5 * HW ** (-0.5)

    def take_in(b, half):
        for i in range(PER):
            rows_in, tags_in = arrival(b * PER + i)
            if i == SELF_PLACE:
                @pl.when(b != core)
                def _():
                    rows_in.wait_recv()
                    tags_in.wait_recv()

                @pl.when(b == core)
                def _():
                    self_copy.wait()
                    self_tag.wait()
            else:
                rows_in.wait_recv()
                tags_in.wait_recv()
        tags = jnp.concatenate(
            [
                jnp.where(low, tag_recv[b * PER], tag_recv[b * PER + 1]),
                jnp.where(low, tag_recv[b * PER + 2], tag_recv[b * PER + 3]),
            ],
            axis=1,
        )
        mask[:, half * BATCH : (half + 1) * BATCH] = (user_mat[...] == tags).astype(jnp.float32)

    def project_head(h, first, count):
        rows = pl.ds(pl.multiple_of(first, BATCH), count)
        kv_ref[h, :count] = silu_half(
            0.5 * jnp.dot(recv[rows, :], kv_w[h], preferred_element_type=jnp.float32)
        ).astype(jnp.bfloat16)

    def attend_head(h, count):
        half = scale * lax.dot_general(
            q_all[:, h * HW : (h + 1) * HW], kv_ref[h, :count, :HW], (((1,), (1,)), ((), ())),
            preferred_element_type=jnp.float32,
        )
        weight = (silu_half(half) * mask[:, :count]).astype(jnp.bfloat16)
        return total[h] + jnp.dot(
            weight, kv_ref[h, :count, HW:], preferred_element_type=jnp.float32
        )

    def batch(b, carry):
        take_in(b, 0)
        for h in range(HEADS):
            project_head(h, b * BATCH, BATCH)

        @pl.when(b == 0)
        def _():
            for d in range(1, SEQ):
                q_copy(d).wait_recv()

        for h in range(HEADS):
            total[h] = attend_head(h, BATCH)
        return carry

    lax.fori_loop(0, BATCHES - 2, batch, 0)
    shift = total[0]
    for h in range(1, HEADS):
        shift = shift + total[h]
    shift = jnp.sum(shift, axis=1, keepdims=True) * (1.0 / D)
    for h in range(HEADS):
        total[h] = total[h] - shift

    def part_copy(d, n):
        peer = lax.rem(z + d, SEQ)
        cols = pl.ds(n * SLICE * HW, SLICE * HW)
        return pltpu.make_async_remote_copy(
            part_send.at[pl.ds(pl.multiple_of(peer * CAND, CAND), CAND), cols],
            part_recv.at[d, :, cols],
            part_send_sem.at[n * SEQ + d], part_recv_sem.at[n * SEQ + d],
            device_id=(dp, peer), device_id_type=MESH,
        )

    take_in(BATCHES - 2, 0)
    take_in(BATCHES - 1, 1)
    for n in range(SLICES + 1):
        for h in range(n * SLICE, min((n + 1) * SLICE, HEADS)):
            project_head(h, GROUPS * CAP - LAST, LAST)
        if n:
            for h in range((n - 1) * SLICE, n * SLICE):
                head_total = attend_head(h, LAST)
                total[h] = head_total
                part_send[:, h * HW : (h + 1) * HW] = head_total.astype(jnp.bfloat16)
            for d in (4, 3, 5, 2, 6, 1, 7):
                part_copy(d, n - 1).start()

    load_out.wait()
    slices = []
    for n in range(SLICES):
        heads = range(n * SLICE, (n + 1) * SLICE)
        some = jnp.concatenate([total[h, own_rows, :] for h in heads], axis=1)
        for d in (1, 7, 2, 6, 3, 5, 4):
            part_copy(d, n).wait_recv()
            some = some + part_recv[d, :, n * SLICE * HW : (n + 1) * SLICE * HW].astype(jnp.float32)
        slices.append(some)
    attended = jnp.concatenate(slices, axis=1)
    mean = jnp.mean(attended, axis=1, keepdims=True)
    centered = attended - mean
    variance = jnp.mean(centered * centered, axis=1, keepdims=True)
    normed = centered * lax.rsqrt(variance + 1e-06)
    gated = (normed * qu[:, D:].astype(jnp.float32)).astype(jnp.bfloat16)
    for c in range(D // 256):
        cols = slice(c * 256, (c + 1) * 256)
        out_ref[:, cols] = candidates[:, cols].astype(jnp.float32) + jnp.dot(
            gated, out_w[:, cols], preferred_element_type=jnp.float32
        )

    def drain(j, carry):
        for i in range(PER):
            if i == SELF_PLACE:
                @pl.when(j != self_part)
                def _():
                    row_copy(j, i).wait_send()
                    tag_copy(j, i).wait_send()
            else:
                row_copy(j, i).wait_send()
                tag_copy(j, i).wait_send()
        return carry

    lax.fori_loop(0, BATCHES, drain, 0)
    for d in range(1, SEQ):
        q_copy(d).wait_send()
        for n in range(SLICES):
            part_copy(d, n).wait_send()


def on_device(history, hist_dest, hist_user, candidates, cand_user, w_qu, w_kv, w_out):
    vmem = pl.BlockSpec(memory_space=pltpu.VMEM)
    hbm = pl.BlockSpec(memory_space=pl.ANY)
    dma = pltpu.SemaphoreType.DMA
    bf16, f32 = jnp.bfloat16, jnp.float32
    return pl.pallas_call(
        kernel,
        out_shape=jax.ShapeDtypeStruct((CAND, D), f32),
        in_specs=[hbm, vmem, vmem, vmem, vmem, hbm, hbm, hbm],
        out_specs=vmem,
        scratch_shapes=[
            pltpu.VMEM((ROWS, D), bf16),
            pltpu.VMEM((D, 2 * D), bf16),
            pltpu.VMEM((HEADS, D, 2 * HW), bf16),
            pltpu.VMEM((D, D), bf16),
            pltpu.VMEM((GROUPS * CAP, D), bf16),
            pltpu.VMEM((GROUPS * CAP, D), bf16),
            pltpu.VMEM((2 * BATCHES, 1, 128), f32),
            pltpu.VMEM((GROUPS, 1, 128), f32),
            pltpu.VMEM((1, ROWS), jnp.int32),
            pltpu.VMEM((CAND, 2 * D), bf16),
            pltpu.VMEM((GROUP_CAND, D), bf16),
            pltpu.VMEM((GROUP_CAND, BATCH), f32),
            pltpu.VMEM((GROUP_CAND, LAST), f32),
            pltpu.VMEM((HEADS, LAST, 2 * HW), bf16),
            pltpu.VMEM((HEADS, GROUP_CAND, HW), f32),
            pltpu.VMEM((GROUP_CAND, D), bf16),
            pltpu.VMEM((SEQ, CAND, D), bf16),
            dma((6,)),
            dma((2 * HEADS,)),
            dma((GROUPS,)),
            dma((GROUPS,)),
            dma((GROUPS,)),
            dma((GROUPS,)),
            dma((SEQ,)),
            dma((SEQ,)),
            dma((SEQ * SLICES,)),
            dma((SEQ * SLICES,)),
            dma((2,)),
        ],
        compiler_params=pltpu.CompilerParams(
            collective_id=0, has_side_effects=True, vmem_limit_bytes=56 << 20
        ),
        name="route_attend_score",
    )(
        history, hist_dest.reshape(1, ROWS), hist_user.reshape(1, ROWS), candidates,
        cand_user.reshape(1, GROUP_CAND), w_qu, w_kv, w_out,
    )


def solution(mesh):
    placed = (
        P(("dp", "seq"), None),
        P(("dp", "seq"), None),
        P(("dp", "seq")),
        P(("dp", "seq"), None),
        P("dp"),
        P(),
        P(),
        P(),
    )
    return jax.shard_map(
        on_device, mesh=mesh, in_specs=placed, out_specs=P(("dp", "seq"), None), check_vma=False
    )
```

```python
import functools

import jax
import jax.numpy as jnp
from jax import lax
from jax.experimental import pallas as pl
from jax.experimental.pallas import tpu as pltpu
from jax.sharding import PartitionSpec as P

D = 1024
HEADS = 8
HW = D // HEADS
ROWS = 1024
GROUPS = 32
SEQ = 8
CAP = 2 * ROWS // GROUPS
CAND = 32
GROUP_CAND = CAND * SEQ
PER = 4
BATCH = PER * CAP
BATCHES = GROUPS // PER
MESH = pl.DeviceIdType.MESH
PACKED_FIRST = 2
SELF_PLACE = 3
ORDER = (0, 1, 4, 2, 3, 5, 6, 7)
LAST = 2 * BATCH
SLICE = 2
SLICES = HEADS // SLICE


def silu_half(half):
    return half + half * jnp.tanh(half)


def kernel(
    history, dest_ref, user_ref, candidates, cand_user, w_qu, w_kv, w_out, out_ref,
    hist, qu_w, kv_w, out_w, send, recv, tag_send, tag_recv, slot_ref, qu, q_all, user_mat,
    mask, kv_ref, total, part_send, part_recv,
    load_sem, kv_sem, send_sem, recv_sem, tag_send_sem, tag_recv_sem, q_send_sem, q_recv_sem,
    part_send_sem, part_recv_sem, self_sem,
):
    dp = lax.axis_index("dp")
    z = lax.axis_index("seq")
    core = lax.rem(dp, 2)
    y = lax.rem(lax.div(dp, 2), 4)
    x = lax.div(dp, 8)
    sign = 1 - 2 * core

    step = ROWS // 4
    load_hist = [
        pltpu.make_async_copy(
            history.at[pl.ds(c * step, step)], hist.at[pl.ds(c * step, step)], load_sem.at[c]
        )
        for c in range(4)
    ]
    load_qu = pltpu.make_async_copy(w_qu, qu_w, load_sem.at[4])
    load_out = pltpu.make_async_copy(w_out, out_w, load_sem.at[5])
    for copy in load_hist:
        copy.start()

    barrier = pltpu.get_barrier_semaphore()
    for other in range(1, GROUPS):
        pl.semaphore_signal(
            barrier, inc=1, device_id=(lax.rem(dp + other, GROUPS), z), device_id_type=MESH
        )
    for d in range(1, SEQ):
        pl.semaphore_signal(
            barrier, inc=1, device_id=(dp, lax.rem(z + d, SEQ)), device_id_type=MESH
        )

    def kv_copies(h):
        cols = pl.ds(h * HW, HW)
        cols_v = pl.ds(D + h * HW, HW)
        return (
            pltpu.make_async_copy(w_kv.at[:, cols], kv_w.at[h, :, pl.ds(0, HW)], kv_sem.at[2 * h]),
            pltpu.make_async_copy(
                w_kv.at[:, cols_v], kv_w.at[h, :, pl.ds(HW, HW)], kv_sem.at[2 * h + 1]
            ),
        )

    blocks = ROWS // 128
    group_ids = lax.broadcasted_iota(jnp.int32, (GROUPS, 128), 0)
    members = [
        (dest_ref[:, b * 128 : (b + 1) * 128] == group_ids).astype(jnp.float32)
        for b in range(blocks)
    ]
    upper = (
        lax.broadcasted_iota(jnp.int32, (128, 128), 0)
        <= lax.broadcasted_iota(jnp.int32, (128, 128), 1)
    ).astype(jnp.float32)
    running = jnp.dot(
        jnp.concatenate(members, axis=0).astype(jnp.bfloat16),
        upper.astype(jnp.bfloat16),
        preferred_element_type=jnp.float32,
    )
    before = jnp.zeros((GROUPS, 1), jnp.float32)
    for b in range(blocks):
        inside = running[b * GROUPS : (b + 1) * GROUPS]
        rank = jnp.sum(members[b] * (inside + (before - 1.0)), axis=0, keepdims=True)
        slot_ref[:, b * 128 : (b + 1) * 128] = (
            dest_ref[:, b * 128 : (b + 1) * 128] * CAP + rank.astype(jnp.int32)
        )
        before = before + inside[:, 127:128]

    for copy in load_hist:
        copy.wait()
    load_qu.start()
    for h in range(HEADS):
        for copy in kv_copies(h):
            copy.start()
    load_out.start()

    def target(j, i):
        jj = lax.rem(j, 4)
        a = jnp.where((j == 2) | (j == 5), 2, 1)
        b = jnp.where((j == 3) | (j == 6), 0, 1)
        dx, dy = ((a, b), (-b, a), (-a, -b), (b, -a))[i]
        dx = jnp.where(jj == 0, 2 * (1 - i % 2), dx)
        dy = jnp.where(jj == 0, 2 * (1 - i // 2), dy)
        to_x = lax.rem(x + sign * dx + 4, 4)
        to_y = lax.rem(y + sign * dy + 4, 4)
        return to_x * 8 + to_y * 2 + lax.div(j, 4)

    def block(k):
        return pl.ds(pl.multiple_of(k * CAP, CAP), CAP)

    def row_copy(j, i):
        k = j * PER + i
        r = lax.rem(j, 4) * 2 * PER + core * PER + i
        return pltpu.make_async_remote_copy(
            send.at[block(k)], recv.at[block(r)], send_sem.at[k], recv_sem.at[r],
            device_id=(target(j, i), z), device_id_type=MESH,
        )

    def tag_copy(j, i):
        k = j * PER + i
        r = lax.rem(j, 4) * 2 * PER + core * PER + i
        return pltpu.make_async_remote_copy(
            tag_send.at[2 * j + i // 2], tag_recv.at[r], tag_send_sem.at[k], tag_recv_sem.at[r],
            device_id=(target(j, i), z), device_id_type=MESH,
        )

    def arrival(r):
        return (
            pltpu.make_async_remote_copy(
                send.at[block(r)], recv.at[block(r)], send_sem.at[r], recv_sem.at[r],
                device_id=(dp, lax.rem(z + 1, SEQ)), device_id_type=MESH,
            ),
            pltpu.make_async_remote_copy(
                tag_send.at[0], tag_recv.at[r], tag_send_sem.at[r], tag_recv_sem.at[r],
                device_id=(dp, lax.rem(z + 1, SEQ)), device_id_type=MESH,
            ),
        )

    self_part = core * 4
    self_copy = pltpu.make_async_copy(
        send.at[block(self_part * PER + SELF_PLACE)], recv.at[block(core * PER + SELF_PLACE)],
        self_sem.at[0],
    )
    self_tag = pltpu.make_async_copy(
        tag_send.at[2 * self_part + SELF_PLACE // 2], tag_recv.at[core * PER + SELF_PLACE],
        self_sem.at[1],
    )

    users = user_ref[...].astype(jnp.float32).astype(jnp.bfloat16)
    users = jnp.broadcast_to(users, (16, ROWS))
    slot_row = slot_ref[...]

    def pack(j):
        inside = lax.broadcasted_iota(jnp.int32, (CAP, ROWS), 0)
        picks = jnp.concatenate(
            [
                ((slot_row - target(j, i) * CAP) == inside).astype(jnp.float32)
                for i in range(PER)
            ],
            axis=0,
        ).astype(jnp.bfloat16)
        tags = lax.dot_general(
            users, picks, (((1,), (1,)), ((), ())), preferred_element_type=jnp.float32
        )
        tag_send[2 * j] = tags[0:1, 0:128]
        tag_send[2 * j + 1] = tags[0:1, 128:256]
        rows = pl.ds(pl.multiple_of(j * BATCH, BATCH), BATCH)
        for c in range(D // 256):
            send[rows, c * 256 : (c + 1) * 256] = jnp.dot(
                picks, hist[:, c * 256 : (c + 1) * 256], preferred_element_type=jnp.float32
            ).astype(jnp.bfloat16)

    def dispatch(j):
        for i in range(PER):
            if i == SELF_PLACE:
                @pl.when(j != self_part)
                def _():
                    row_copy(j, i).start()
                    tag_copy(j, i).start()

                @pl.when(j == self_part)
                def _():
                    self_copy.start()
                    self_tag.start()
            else:
                row_copy(j, i).start()
                tag_copy(j, i).start()

    def part_at(place):
        part = place
        for at, value in enumerate(ORDER):
            part = jnp.where(place == at, value, part)
        return part

    def dispatch_and_pack(j, carry):
        dispatch(part_at(j))
        pack(part_at(j + 1))
        return carry

    pack(ORDER[0])
    pl.semaphore_wait(barrier, GROUPS - 1 + SEQ - 1)
    lax.fori_loop(0, PACKED_FIRST, dispatch_and_pack, 0)

    load_qu.wait()

    for c in range(2 * D // 256):
        cols = slice(c * 256, (c + 1) * 256)
        qu[:, cols] = silu_half(
            0.5 * jnp.dot(candidates[...], qu_w[:, cols], preferred_element_type=jnp.float32)
        ).astype(jnp.bfloat16)
    own_rows = pl.ds(pl.multiple_of(z * CAND, CAND), CAND)
    q_all[own_rows, :] = qu[:, :D]

    def q_copy(d):
        return pltpu.make_async_remote_copy(
            qu.at[:, pl.ds(0, D)], q_all.at[own_rows], q_send_sem.at[d], q_recv_sem.at[d],
            device_id=(dp, lax.rem(z + d, SEQ)), device_id_type=MESH,
        )

    for d in range(1, SEQ):
        q_copy(d).start()
    lax.fori_loop(PACKED_FIRST, BATCHES - 1, dispatch_and_pack, 0)
    dispatch(ORDER[-1])

    square = (
        lax.broadcasted_iota(jnp.int32, (GROUP_CAND, GROUP_CAND), 0)
        == lax.broadcasted_iota(jnp.int32, (GROUP_CAND, GROUP_CAND), 1)
    )
    cand_col = jnp.sum(
        jnp.where(square, cand_user[...].astype(jnp.float32), 0.0), axis=1, keepdims=True
    )
    user_mat[...] = jnp.broadcast_to(cand_col, (GROUP_CAND, BATCH))
    total[...] = jnp.zeros_like(total)

    for h in range(HEADS):
        for copy in kv_copies(h):
            copy.wait()

    low = lax.broadcasted_iota(jnp.int32, (1, 128), 1) < CAP
    scale = 0.5 * HW ** (-0.5)

    def take_in(b, half):
        for i in range(PER):
            rows_in, tags_in = arrival(b * PER + i)
            if i == SELF_PLACE:
                @pl.when(b != core)
                def _():
                    rows_in.wait_recv()
                    tags_in.wait_recv()

                @pl.when(b == core)
                def _():
                    self_copy.wait()
                    self_tag.wait()
            else:
                rows_in.wait_recv()
                tags_in.wait_recv()
        tags = jnp.concatenate(
            [
                jnp.where(low, tag_recv[b * PER], tag_recv[b * PER + 1]),
                jnp.where(low, tag_recv[b * PER + 2], tag_recv[b * PER + 3]),
            ],
            axis=1,
        )
        mask[:, half * BATCH : (half + 1) * BATCH] = (user_mat[...] == tags).astype(jnp.float32)

    def project_head(h, first, count):
        rows = pl.ds(pl.multiple_of(first, BATCH), count)
        kv_ref[h, :count] = silu_half(
            0.5 * jnp.dot(recv[rows, :], kv_w[h], preferred_element_type=jnp.float32)
        ).astype(jnp.bfloat16)

    def attend_head(h, count):
        half = scale * lax.dot_general(
            q_all[:, h * HW : (h + 1) * HW], kv_ref[h, :count, :HW], (((1,), (1,)), ((), ())),
            preferred_element_type=jnp.float32,
        )
        weight = (silu_half(half) * mask[:, :count]).astype(jnp.bfloat16)
        return total[h] + jnp.dot(
            weight, kv_ref[h, :count, HW:], preferred_element_type=jnp.float32
        )

    def batch(b, carry):
        take_in(b, 0)
        for h in range(HEADS):
            project_head(h, b * BATCH, BATCH)

        @pl.when(b == 0)
        def _():
            for d in range(1, SEQ):
                q_copy(d).wait_recv()

        for h in range(HEADS):
            total[h] = attend_head(h, BATCH)
        return carry

    lax.fori_loop(0, BATCHES - 2, batch, 0)
    shift = total[0]
    for h in range(1, HEADS):
        shift = shift + total[h]
    shift = jnp.sum(shift, axis=1, keepdims=True) * (1.0 / D)
    for h in range(HEADS):
        total[h] = total[h] - shift

    def part_copy(d, n):
        peer = lax.rem(z + d, SEQ)
        cols = pl.ds(n * SLICE * HW, SLICE * HW)
        return pltpu.make_async_remote_copy(
            part_send.at[pl.ds(pl.multiple_of(peer * CAND, CAND), CAND), cols],
            part_recv.at[d, :, cols],
            part_send_sem.at[n * SEQ + d], part_recv_sem.at[n * SEQ + d],
            device_id=(dp, peer), device_id_type=MESH,
        )

    take_in(BATCHES - 2, 0)
    take_in(BATCHES - 1, 1)
    for n in range(SLICES + 1):
        for h in range(n * SLICE, min((n + 1) * SLICE, HEADS)):
            project_head(h, GROUPS * CAP - LAST, LAST)
        if n:
            for h in range((n - 1) * SLICE, n * SLICE):
                head_total = attend_head(h, LAST)
                total[h] = head_total
                part_send[:, h * HW : (h + 1) * HW] = head_total.astype(jnp.bfloat16)
            for d in (4, 3, 5, 2, 6, 1, 7):
                part_copy(d, n - 1).start()

    load_out.wait()
    slices = []
    for n in range(SLICES):
        heads = range(n * SLICE, (n + 1) * SLICE)
        some = jnp.concatenate([total[h, own_rows, :] for h in heads], axis=1)
        for d in (1, 7, 2, 6, 3, 5, 4):
            part_copy(d, n).wait_recv()
            some = some + part_recv[d, :, n * SLICE * HW : (n + 1) * SLICE * HW].astype(jnp.float32)
        slices.append(some)
    attended = jnp.concatenate(slices, axis=1)
    mean = jnp.mean(attended, axis=1, keepdims=True)
    centered = attended - mean
    variance = jnp.mean(centered * centered, axis=1, keepdims=True)
    normed = centered * lax.rsqrt(variance + 1e-06)
    gated = (normed * qu[:, D:].astype(jnp.float32)).astype(jnp.bfloat16)
    for c in range(D // 256):
        cols = slice(c * 256, (c + 1) * 256)
        out_ref[:, cols] = candidates[:, cols].astype(jnp.float32) + jnp.dot(
            gated, out_w[:, cols], preferred_element_type=jnp.float32
        )

    def drain(j, carry):
        for i in range(PER):
            if i == SELF_PLACE:
                @pl.when(j != self_part)
                def _():
                    row_copy(j, i).wait_send()
                    tag_copy(j, i).wait_send()
            else:
                row_copy(j, i).wait_send()
                tag_copy(j, i).wait_send()
        return carry

    lax.fori_loop(0, BATCHES, drain, 0)
    for d in range(1, SEQ):
        q_copy(d).wait_send()
        for n in range(SLICES):
            part_copy(d, n).wait_send()


def on_device(history, hist_dest, hist_user, candidates, cand_user, w_qu, w_kv, w_out):
    vmem = pl.BlockSpec(memory_space=pltpu.VMEM)
    hbm = pl.BlockSpec(memory_space=pl.ANY)
    dma = pltpu.SemaphoreType.DMA
    bf16, f32 = jnp.bfloat16, jnp.float32
    return pl.pallas_call(
        kernel,
        out_shape=jax.ShapeDtypeStruct((CAND, D), f32),
        in_specs=[hbm, vmem, vmem, vmem, vmem, hbm, hbm, hbm],
        out_specs=vmem,
        scratch_shapes=[
            pltpu.VMEM((ROWS, D), bf16),
            pltpu.VMEM((D, 2 * D), bf16),
            pltpu.VMEM((HEADS, D, 2 * HW), bf16),
            pltpu.VMEM((D, D), bf16),
            pltpu.VMEM((GROUPS * CAP, D), bf16),
            pltpu.VMEM((GROUPS * CAP, D), bf16),
            pltpu.VMEM((2 * BATCHES, 1, 128), f32),
            pltpu.VMEM((GROUPS, 1, 128), f32),
            pltpu.VMEM((1, ROWS), jnp.int32),
            pltpu.VMEM((CAND, 2 * D), bf16),
            pltpu.VMEM((GROUP_CAND, D), bf16),
            pltpu.VMEM((GROUP_CAND, BATCH), f32),
            pltpu.VMEM((GROUP_CAND, LAST), f32),
            pltpu.VMEM((HEADS, LAST, 2 * HW), bf16),
            pltpu.VMEM((HEADS, GROUP_CAND, HW), f32),
            pltpu.VMEM((GROUP_CAND, D), bf16),
            pltpu.VMEM((SEQ, CAND, D), bf16),
            dma((6,)),
            dma((2 * HEADS,)),
            dma((GROUPS,)),
            dma((GROUPS,)),
            dma((GROUPS,)),
            dma((GROUPS,)),
            dma((SEQ,)),
            dma((SEQ,)),
            dma((SEQ * SLICES,)),
            dma((SEQ * SLICES,)),
            dma((2,)),
        ],
        compiler_params=pltpu.CompilerParams(
            collective_id=0, has_side_effects=True, vmem_limit_bytes=56 << 20
        ),
        name="route_attend_score",
    )(
        history, hist_dest.reshape(1, ROWS), hist_user.reshape(1, ROWS), candidates,
        cand_user.reshape(1, GROUP_CAND), w_qu, w_kv, w_out,
    )


def solution(mesh):
    placed = (
        P(("dp", "seq"), None),
        P(("dp", "seq"), None),
        P(("dp", "seq")),
        P(("dp", "seq"), None),
        P("dp"),
        P(),
        P(),
        P(),
    )
    return jax.shard_map(
        on_device, mesh=mesh, in_specs=placed, out_specs=P(("dp", "seq"), None), check_vma=False
    )
```
